128 devices in a mesh: seq: 4 (over z), head: 32 (over y, x, core).
Axes of the slice: x: 4, y: 4, z: 4, core: 2. Of those that a mesh axis runs over, the one named last changes fastest.
Arguments:
- queries: float32 [8192, 4096], P('seq', 'head'), may hold values from -6 to 6
- key_rows: float32 [8192, 4096], P('seq', 'head'), may hold values from -6 to 6
- values: float32 [8192, 4096], P('seq', 'head'), may hold values from -6 to 6
- out_weight: bfloat16 [4096, 2048], P('head'), may hold values from -0.09375 to 0.09375
- expert_ids: int32 [8192, 8], P(('seq', 'head')), may hold values from 0 to 127, all different within a row; in each aligned block of 64 rows (0 to 63, 64 to 127, ...) at most 8 rows name the same one
- gate_ints: int32 [8192, 8], P(('seq', 'head')), may hold values from 1 to 1023
- w_gate: bfloat16 [128, 2048, 768], P(('seq', 'head')), may hold values from -0.125 to 0.125
- w_up: bfloat16 [128, 2048, 768], P(('seq', 'head')), may hold values from -0.125 to 0.125
- w_down: bfloat16 [128, 768, 2048], P(('seq', 'head')), may hold values from -0.21875 to 0.21875
Outputs:
- layer_out: float32 [8192, 2048], P(('seq', 'head'))
The draws below stay inside these ranges and needn't reach their ends.
Inputs may be any that keep to these rules, and one draw needn't show every extreme that they name: `expert_ids`: each row names 8 different experts. Within the rows of one device (aligned blocks of 64 rows) no expert is named more than 8 times, a bound that some block reaches.
All inputs are finite; a program needn't handle non-finite values.
Results may differ from the reference program's by a relative error of at most 0.017.
Values may be sent and summed in bfloat16 or wider, within the bound.
A program may use at most 128 MiB of HBM per device.

```python
import math
import jax
import jax.numpy as jnp
import numpy as np
from jax import lax

D = 2048
FF = 768
HEADS = 32
DH = 128
TOP = 8
TOK_DEV = 64
EXPERTS = 128
LENGTH = 8192
TOKENS = 8192
CAP = 8
N_SEQ = 4
N_HEAD = 32


def set_ends(values, stream_key, low, top_value):
    place = [jax.random.randint(jax.random.fold_in(stream_key, axis), (), 0, length) for axis, length in enumerate(values.shape)]
    widest = values.shape.index(max(values.shape))
    next_to = place[:widest] + [(place[widest] + 1) % values.shape[widest]] + place[widest + 1:]
    return values.at[tuple(place)].set(low).at[tuple(next_to)].set(top_value)


def steps_of(key, shape, cuts, least, top_value):
    gain = 1.0
    for position, parts in cuts:
        heights = jax.random.uniform(jax.random.fold_in(jax.random.fold_in(key, 6), position), (parts,), jnp.float32, least / len(cuts), top_value / len(cuts))
        gain = gain * jnp.repeat(jnp.exp(heights), shape[position] // parts).reshape((-1,) + (1,) * (len(shape) - 1 - position))
    return gain


def deal_out(rng, own, number, rows, number_of, top, reach, skew):
    order = jax.random.permutation(rng, number_of)
    heavy_load, common = load_shares(number_of, rows * top, reach, skew, True), load_shares(number_of, rows * top, reach, skew, False)
    places = jnp.arange(number_of)

    def named(sizes, turn):
        used = int((sizes > 0).sum())
        fixed = max(1, used // 4)
        moved = fixed + (places - fixed + turn * (used - fixed)) % max(1, number_of - fixed)
        return jnp.zeros((number_of,), jnp.int32).at[order[jnp.where(places < fixed, places, moved)]].set(jnp.asarray(sizes, jnp.int32))

    sizes = jnp.where(number % 4 == 0, named(heavy_load, number // 4), named(common, number - number // 4 - 1))
    mixed = jax.random.permutation(jax.random.fold_in(own, 3), number_of)
    giver, receiver = mixed[0:number_of // 2 * 2:2], mixed[1:number_of // 2 * 2:2]
    room = jnp.minimum(sizes[giver] - 1, reach - sizes[receiver]) // 2
    room = jnp.where((giver == order[0]) | (receiver == order[0]) | (sizes[receiver] == 0), 0, jnp.maximum(room, 0))
    moved = jax.random.randint(jax.random.fold_in(own, 4), (number_of // 2,), 0, 1 << 20) % (room + 1)
    sizes = sizes.at[giver].add(-moved).at[receiver].add(moved)
    labels = jnp.searchsorted(jnp.cumsum(sizes), jnp.arange(rows * top), side="right").astype(jnp.int32)
    grid = labels.reshape(top, rows).T
    grid = grid[jax.random.permutation(jax.random.fold_in(own, 1), rows)]
    turn = jax.random.randint(jax.random.fold_in(own, 2), (rows, 1), 0, top)
    return jnp.take_along_axis(grid, (jnp.arange(top)[None, :] + turn) % top, axis=1)


def load_shares(count, total, limit, skew, full):
    weights = [(1 << 20) // math.isqrt(rank ** skew) + 1 for rank in range(1, count + 1)]
    largest = limit if full else min(limit, max(-(-total // count), total * weights[0] // sum(weights)))
    least = 1 if total - largest >= count - 1 else 0
    holding, surplus = [largest] + [least] * (count - 1), total - largest - least * (count - 1)
    while surplus > 0:
        movable = [i for i in range(1, count) if holding[i] < largest] or [i for i in range(1, count) if holding[i] < limit]
        whole, left = sum([weights[i] for i in movable]), surplus
        for i in movable:
            more = min(limit - holding[i], max(1, left * weights[i] // whole), surplus)
            holding[i] = holding[i] + more
            surplus = surplus - more
    return np.array(holding)


def noise(key, extent, deviation, reach, shards=(), kind=jnp.bfloat16):
    drawn = jax.random.normal(key, extent, jnp.float32) * deviation
    if len(shards) > 0:
        drawn = steps_of(key, extent, shards, -0.22, 0.18) * drawn
    return jnp.clip(drawn, min=-reach, max=reach).astype(kind)


def setup_inputs(seed: int = 0) -> dict:
    seeds = jax.random.split(jax.random.key(seed), 10)
    queries = noise(seeds[0], (LENGTH, HEADS * DH), 1.0, 6.0, ((0, 4), (1, 32)), jnp.float32)
    key_rows = noise(seeds[1], (LENGTH, HEADS * DH), 1.0, 6.0, ((0, 4), (1, 32)), jnp.float32)
    values = noise(seeds[2], (LENGTH, HEADS * DH), 1.0, 6.0, ((0, 4), (1, 32)), jnp.float32)
    out_weight = noise(seeds[3], (HEADS * DH, D), (HEADS * DH) ** -0.5, 0.09375, ((0, 32),))
    expert_ids_keys = jax.random.split(jax.random.fold_in(seeds[4], 1), TOKENS // TOK_DEV)
    expert_ids_turns = jax.random.permutation(jax.random.fold_in(seeds[4], 3), TOKENS // TOK_DEV)
    expert_ids = jax.vmap(lambda own, number: deal_out(jax.random.fold_in(seeds[4], 2), own, number, TOK_DEV, EXPERTS, TOP, CAP, 2))(expert_ids_keys, expert_ids_turns).reshape((TOKENS, TOP))
    gate_ints = set_ends(jax.random.randint(seeds[5], (TOKENS, TOP), 1, 1024), jax.random.fold_in(seeds[5], 1), 1, 1023).astype(jnp.int32)
    w_gate = noise(seeds[6], (EXPERTS, D, FF), D ** -0.5, 0.125, ((0, 128),))
    w_up = noise(seeds[7], (EXPERTS, D, FF), D ** -0.5, 0.125, ((0, 128),))
    w_down = noise(seeds[8], (EXPERTS, FF, D), FF ** -0.5, 0.21875, ((0, 128),))
    return {"queries": queries, "key_rows": key_rows, "values": values, "out_weight": out_weight, "expert_ids": expert_ids, "gate_ints": gate_ints, "w_gate": w_gate, "w_up": w_up, "w_down": w_down}


HIGH = lax.Precision.HIGHEST

def causal_linear(query_heads, key_heads, value_heads):
    heads, length, width = query_heads.shape
    block = math.gcd(512, length)
    count = length // block

    def split(array):
        return array.reshape(heads, count, block, width).transpose(1, 0, 2, 3)
    lower = jnp.tril(jnp.ones((block, block), jnp.float32))

    def advance(state, inputs):
        query_block, key_block, value_block = inputs
        scores = jnp.einsum('hid,hjd->hij', query_block, key_block, precision=HIGH) * lower
        output = jnp.einsum('hij,hjd->hid', scores, value_block, precision=HIGH)
        output = output + jnp.einsum('hid,hde->hie', query_block, state, precision=HIGH)
        state = state + jnp.einsum('hjd,hje->hde', key_block, value_block, precision=HIGH)
        return (state, output)
    start = jnp.zeros((heads, width, width), jnp.float32)
    state, outputs = lax.scan(advance, start, (split(query_heads), split(key_heads), split(value_heads)))
    return (outputs.transpose(1, 0, 2, 3).reshape(heads, length, width), state)

def head_norm(mixed):
    return mixed * lax.rsqrt(lax.optimization_barrier(jnp.mean(mixed * mixed, axis=-1, keepdims=True)) + 1e-06)

def reference(queries, key_rows, values, out_weight, expert_ids, gate_ints, w_gate, w_up, w_down):
    length = queries.shape[0]

    def split_heads(array):
        return array.reshape(length, HEADS, DH).transpose(1, 0, 2)
    heads_out, final_state = causal_linear(split_heads(queries), split_heads(key_rows), split_heads(values))
    attn = head_norm(heads_out).transpose(1, 0, 2).reshape(length, HEADS * DH).astype(jnp.bfloat16)
    projected = jnp.dot(attn, out_weight, preferred_element_type=jnp.float32)
    normed = (projected * lax.rsqrt(lax.optimization_barrier(jnp.mean(projected * projected, axis=-1, keepdims=True)) + 1e-06)).astype(jnp.bfloat16)
    gates = gate_ints.astype(jnp.float32)
    gates = gates / lax.optimization_barrier(jnp.sum(gates, axis=-1, keepdims=True))
    flat_ids = expert_ids.reshape(-1)
    flat_gates = gates.reshape(-1)
    count_all = flat_ids.shape[0]
    owner = jnp.arange(count_all, dtype=jnp.int32) // TOP
    slots = CAP * N_SEQ * N_HEAD

    def expert_step(total, inputs):
        expert, gate_mat, up_mat, down_mat = inputs
        chosen = flat_ids == expert
        rank = jnp.cumsum(chosen.astype(jnp.int32), dtype=jnp.int32) - 1
        target = jnp.where(chosen, rank, slots).astype(jnp.int32)
        source = jnp.zeros((slots,), jnp.int32).at[target].set(jnp.arange(count_all, dtype=jnp.int32), mode='drop')
        filled = jnp.arange(slots, dtype=jnp.int32) < jnp.sum(chosen.astype(jnp.int32))
        tokens = owner[source]
        picked = normed[tokens]
        gate_val = jnp.dot(picked, gate_mat, preferred_element_type=jnp.float32)
        up_val = jnp.dot(picked, up_mat, preferred_element_type=jnp.float32)
        act = (jax.nn.silu(gate_val) * up_val).astype(jnp.bfloat16)
        result = jnp.dot(act, down_mat, preferred_element_type=jnp.float32).astype(jnp.bfloat16)
        result = lax.optimization_barrier(result).astype(jnp.float32)
        weight = jnp.where(filled, flat_gates[source], jnp.zeros_like(flat_gates[source]))
        return (total.at[tokens].add(result * weight[:, None]), None)
    moe_sum, unused = lax.scan(expert_step, jnp.zeros((length, D), jnp.float32), (jnp.arange(EXPERTS, dtype=jnp.int32), w_gate, w_up, w_down))
    return projected + moe_sum
```

```python
import functools

import jax
import jax.numpy as jnp
from jax import lax
from jax.experimental import pallas as pl
from jax.experimental.pallas import tpu as pltpu
from jax.sharding import PartitionSpec as P

MESH = pl.DeviceIdType.MESH
BF = jnp.bfloat16
F32 = jnp.float32
COLS = (768, 640, 640)
OFF = (0, 768, 1408)
PLANE = ((1, 2), (0, 2), (0, 1))
ORDER = (5, 10, 2, 8, 15, 7, 13, 1, 4, 11, 14, 3, 12, 6, 9)
CB = 4
CBW = 512
CHUNK = 256


def partners():
    found = []
    for a in range(4):
        for b in range(4):
            for d in range(4):
                if 0 in (a, b, d) and (a, b, d) != (0, 0, 0):
                    found.append((a, b, d, 0))
    found.append((0, 0, 0, 1))
    for a in range(1, 4):
        found += [(a, 0, 0, 1), (0, a, 0, 1), (0, 0, a, 1)]
    return found


def body(
    q_h, k_h, v_h, w_h, ids_ref, gi_ref, wg_h, wu_h, wd_h, out_ref,
    q_s, k_s, v_s, o_s, st_s, st_r, at_s, at_r, w_s, rs_s, rs_r, pf_s, pj_s,
    vg_s, m0, m1, m2, sel_s, com_s, l0, l1, l2, ds0, ds1, ds2, r0, r1, r2,
    o0, o1, o2, rt0, rt1, rt2, ps0, ps1, ps2, pr0, pr1, pr2, wg_s, wu_s, wd_s,
    loc_sem, st_ss, st_rs, at_ss, at_rs, w_ss, w_rs, wf_ss, wf_rs, rs_ss, rs_rs,
    m_ss, m_rs, l_ss, l_rs, d_ss, d_rs, e_ss, e_rs, p_ss, p_rs,
):
    meta, line = (m0, m1, m2), (l0, l1, l2)
    ds, rr, oo, rt = (ds0, ds1, ds2), (r0, r1, r2), (o0, o1, o2), (rt0, rt1, rt2)
    ps, pr = (ps0, ps1, ps2), (pr0, pr1, pr2)
    z = lax.axis_index("seq")
    head = lax.axis_index("head")
    y, x, c = head // 8, (head // 2) % 4, head % 2
    at = (x, y, z)
    other = 1 - c

    def dev(coords, core):
        return (coords[2], (coords[1] * 4 + coords[0]) * 2 + core)

    def moved(**shift):
        return tuple((at[i] + shift.get("xyz"[i], 0)) % 4 for i in range(3))

    def along(axis, d):
        return tuple((at[i] + d) % 4 if i == axis else at[i] for i in range(3))

    sent = []

    def send(src, dst, ss, rs, device):
        copy = pltpu.make_async_remote_copy(
            src_ref=src, dst_ref=dst, send_sem=ss, recv_sem=rs, device_id=device, device_id_type=MESH
        )
        copy.start()
        sent.append(copy)
        return copy

    loads = []
    for i, (src, dst) in enumerate(
        ((k_h, k_s), (v_h, v_s), (q_h, q_s), (w_h, w_s.at[y, c]), (wg_h, wg_s), (wu_h, wu_s), (wd_h, wd_s))
    ):
        copy = pltpu.make_async_copy(src, dst, loc_sem.at[i])
        copy.start()
        loads.append(copy)

    barrier = pltpu.get_barrier_semaphore()
    greeted = partners()
    for dx, dy, dz, dc in greeted:
        core = other if dc else c
        pl.semaphore_signal(
            barrier, inc=1, device_id=dev(moved(x=dx, y=dy, z=dz), core), device_id_type=MESH
        )

    experts = lax.broadcasted_iota(jnp.int32, (64, 128), 1)
    named = jnp.zeros((64, 128), F32)
    gate = jnp.zeros((64, 128), F32)
    gates = gi_ref[...].astype(F32)
    gates = gates / jnp.sum(gates, axis=-1, keepdims=True)
    for k in range(8):
        hit = ids_ref[:, k : k + 1] == experts
        named = jnp.where(hit, 1.0, named)
        gate = jnp.where(hit, gates[:, k : k + 1], gate)
    before = (
        lax.broadcasted_iota(jnp.int32, (64, 64), 1) < lax.broadcasted_iota(jnp.int32, (64, 64), 0)
    ).astype(F32).astype(BF)
    rank = jnp.dot(before, named.astype(BF), preferred_element_type=F32)
    vg_s[:, :128] = jnp.where(named > 0.5, rank, -1.0).astype(BF)
    vg_s[:, 128:] = gate.astype(BF)

    pl.semaphore_wait(barrier, len(greeted))

    meta_in = []
    for p in range(3):
        meta[p][at[p], c] = vg_s[...]
        for i in range(1, 8):
            d, k = i // 2, i % 2
            meta_in.append(
                send(
                    vg_s, meta[p].at[at[p], c], m_ss.at[p * 8 + i], m_rs.at[p * 8 + i],
                    dev(along(p, d), other if k else c),
                )
            )
    loads[3].wait()
    mine = w_s.at[y, c]
    w_in = [send(mine, mine, w_ss.at[d], w_rs.at[d], dev(along(1, d), c)) for d in (2, 1, 3)]
    wf_in = [send(mine, mine, wf_ss.at[0], wf_rs.at[0], dev(at, other))]

    loads[0].wait()
    loads[1].wait()
    count = q_s.shape[0]
    state = jnp.zeros((128, 128), F32)
    prefix = []
    for i in range(count):
        prefix.append(state)
        state = state + lax.dot_general(
            k_s[i].astype(BF), v_s[i].astype(BF), (((0,), (0,)), ((), ())), preferred_element_type=F32
        )
    st_s[...] = state.astype(BF)
    st_in = [
        send(st_s, st_r.at[z], st_ss.at[d], st_rs.at[d], dev(along(2, d), c)) for d in (1, 2, 3)
    ]
    loads[2].wait()
    lower = lax.broadcasted_iota(jnp.int32, (CHUNK, CHUNK), 1) <= lax.broadcasted_iota(
        jnp.int32, (CHUNK, CHUNK), 0
    )
    for i in range(count):
        qb, kb = q_s[i].astype(BF), k_s[i].astype(BF)
        scores = lax.dot_general(qb, kb, (((1,), (1,)), ((), ())), preferred_element_type=F32)
        scores = jnp.where(lower, scores, 0.0).astype(BF)
        o_s[i] = jnp.dot(scores, v_s[i].astype(BF), preferred_element_type=F32)
    for copy in st_in:
        copy.wait_recv()
    earlier = jnp.zeros((128, 128), F32)
    for d in (1, 2, 3):
        source = (z - d + 4) % 4
        earlier = earlier + jnp.where(source < z, st_r[source].astype(F32), 0.0)
    for i in range(count):
        total = (prefix[i] + earlier).astype(BF)
        mixed = o_s[i] + jnp.dot(q_s[i].astype(BF), total, preferred_element_type=F32)
        mixed = mixed * lax.rsqrt(jnp.mean(mixed * mixed, axis=-1, keepdims=True) + 1e-06)
        mixed = mixed.astype(BF)
        for j in range(2):
            for k in range(2):
                at_s[i // 2, k, (i % 2) * 2 + j] = mixed[(2 * j + k) * 64 : (2 * j + k + 1) * 64]
    at_in = []
    for i in (4, 5, 2, 3, 6, 7, 1):
        d, k = i // 2, i % 2
        to = (y + d) % 4
        core = other if k else c
        at_in.append(
            send(at_s.at[to, core], at_r.at[y, c], at_ss.at[i], at_rs.at[i], dev(along(1, d), core))
        )
    at_r[y, c] = at_s[y, c]

    for copy in meta_in:
        copy.wait_recv()
    row_e = lax.broadcasted_iota(jnp.int32, (128, 256), 0)
    col_r = lax.broadcasted_iota(jnp.int32, (128, 256), 1)
    first, second = col_r // 64, (col_r // 16) % 4
    same = (row_e // 64) == ((col_r // 8) % 2)
    slot = jnp.where(same, (col_r % 8).astype(F32), -2.0)
    for p in range(3):
        if p == 0:
            expert = second * 32 + first * 8 + x * 2 + c
        elif p == 1:
            expert = second * 32 + y * 8 + first * 2 + c
        else:
            expert = z * 32 + second * 8 + first * 2 + c
        spread = (row_e == expert).astype(F32).astype(BF)

        def make(a, carry, p=p, spread=spread):
            both = meta[p][a].reshape(128, 256)
            ranks = jnp.dot(both[:, :128], spread, preferred_element_type=F32)
            weight = jnp.dot(both[:, 128:], spread, preferred_element_type=F32)
            hit = ranks == slot
            com_s[p, a] = jnp.where(hit, weight, 0.0).astype(BF)
            sel_s[p, a] = jnp.where(hit, 1.0, 0.0).T.astype(BF)
            return carry

        lax.fori_loop(0, 4, make, 0)

    for copy, d in zip(w_in, (2, 1, 3)):
        copy.wait_recv()
        got = w_s.at[(y - d + 4) % 4, c]
        wf_in.append(send(got, got, wf_ss.at[d], wf_rs.at[d], dev(at, other)))
    for copy in at_in:
        copy.wait_recv()
    for copy in wf_in:
        copy.wait_recv()
    lhs = jnp.concatenate(
        [at_r[i // 2, i % 2].reshape(256, 128) for i in range(8)], axis=1
    )
    rs_in = []
    for b in range(CB):
        part = jnp.dot(
            lhs, w_s[:, :, :, b * CBW : (b + 1) * CBW].reshape(1024, CBW), preferred_element_type=F32
        ).reshape(4, 64, CBW)
        pf_s[b] = part
        rs_s[b] = part.astype(BF)
        for d in (2, 1, 3):
            i = b * 4 + d
            rs_in.append(
                send(rs_s.at[b, (x + d) % 4], rs_r.at[b, x], rs_ss.at[i], rs_rs.at[i], dev(along(0, d), c))
            )
    for copy in rs_in:
        copy.wait_recv()
    square = jnp.zeros((64, 1), F32)
    for b in range(CB):
        total = pf_s[b, x]
        for d in (1, 2, 3):
            total = total + rs_r[b, (x - d + 4) % 4].astype(F32)
        pj_s[:, b * CBW : (b + 1) * CBW] = total
        square = square + jnp.sum(total * total, axis=-1, keepdims=True)
    scale = lax.rsqrt(square / 2048.0 + 1e-06)

    line_in = {}
    for p in range(3):
        line[p][at[p], c] = (pj_s[:, OFF[p] : OFF[p] + COLS[p]] * scale).astype(BF)
    for i in (1, 2, 6, 3, 7, 4, 5):
        d, k = i // 2, i % 2
        for p in range(3):
            own = line[p].at[at[p], c]
            line_in[p, i] = send(
                own, own, l_ss.at[p * 8 + i], l_rs.at[p * 8 + i], dev(along(p, d), other if k else c)
            )
    for d in (0, 1, 3, 2):
        for p in range(3):
            source = (at[p] - d + 4) % 4
            for k in range(2):
                if (d, k) != (0, 0):
                    line_in[p, d * 2 + k].wait_recv()
            picked = jnp.dot(
                sel_s[p, source], line[p][source].reshape(128, COLS[p]), preferred_element_type=F32
            )
            ds[p][source] = picked.astype(BF).reshape(16, 16, COLS[p])

    def across(ref, p, first, second):
        return (
            ref.at[:, first, second] if p == 0 else ref.at[first, :, second] if p == 1 else ref.at[first, second]
        )

    d_in = []
    own_copies = []
    here = [(at[PLANE[p][0]], at[PLANE[p][1]]) for p in range(3)]
    for p in range(3):
        copy = pltpu.make_async_copy(
            ds[p].at[:, here[p][0] * 4 + here[p][1]], across(rr[p], p, *here[p]), d_rs.at[p * 16]
        )
        copy.start()
        own_copies.append(copy)

    def plane_target(p, i):
        a, b = i // 4, i % 4
        first, second = (here[p][0] + a) % 4, (here[p][1] + b) % 4
        coords = [None] * 3
        coords[p] = at[p]
        coords[PLANE[p][0]], coords[PLANE[p][1]] = first, second
        return first, second, dev(coords, c)

    for i in ORDER:
        for p in range(3):
            first, second, device = plane_target(p, i)
            d_in.append(
                send(
                    ds[p].at[:, first * 4 + second], across(rr[p], p, *here[p]),
                    d_ss.at[p * 16 + i], d_rs.at[p * 16 + i], device,
                )
            )
    for copy in loads[4:]:
        copy.wait()
    for copy in own_copies:
        copy.wait()
    for copy in d_in:
        copy.wait_recv()

    def expert_rows(step, carry):
        block = (x + step) % 4
        rows = [rr[p][block].reshape(256, COLS[p]) for p in range(3)]
        gate_val = jnp.zeros((256, 768), F32)
        up_val = jnp.zeros((256, 768), F32)
        for p in range(3):
            gate_val = gate_val + jnp.dot(
                rows[p], wg_s[OFF[p] : OFF[p] + COLS[p]], preferred_element_type=F32
            )
            up_val = up_val + jnp.dot(
                rows[p], wu_s[OFF[p] : OFF[p] + COLS[p]], preferred_element_type=F32
            )
        act = (gate_val / (1.0 + jnp.exp(-gate_val)) * up_val).astype(BF)
        for p in range(3):
            result = jnp.dot(act, wd_s[:, OFF[p] : OFF[p] + COLS[p]], preferred_element_type=F32)
            oo[p][block] = result.astype(BF).reshape(4, 4, 16, COLS[p])
        return carry

    lax.fori_loop(0, 4, expert_rows, 0)

    own_copies = []
    e_in = []
    for p in range(3):
        copy = pltpu.make_async_copy(
            across(oo[p], p, *here[p]), rt[p].at[:, here[p][0] * 4 + here[p][1]], e_rs.at[p * 16]
        )
        copy.start()
        own_copies.append(copy)
    for i in ORDER:
        for p in range(3):
            first, second, device = plane_target(p, i)
            e_in.append(
                send(
                    across(oo[p], p, first, second), rt[p].at[:, here[p][0] * 4 + here[p][1]],
                    e_ss.at[p * 16 + i], e_rs.at[p * 16 + i], device,
                )
            )
    for copy in own_copies:
        copy.wait()
    for copy in e_in:
        copy.wait_recv()

    p_in = []
    for d in (2, 1, 3, 0):
        for p in range(3):
            to = (at[p] + d) % 4
            sums = jnp.dot(
                com_s[p, to], rt[p][to].reshape(256, COLS[p]), preferred_element_type=F32
            )
            ps[p][to] = sums.astype(BF).reshape(2, 64, COLS[p])
            for k in range(2):
                if (d, k) != (0, 0):
                    i = d * 2 + k
                    core = other if k else c
                    p_in.append(
                        send(
                            ps[p].at[to, core], pr[p].at[at[p], c], p_ss.at[p * 8 + i], p_rs.at[p * 8 + i],
                            dev(along(p, d), core),
                        )
                    )
    for p in range(3):
        pr[p][at[p], c] = ps[p][at[p], c]
    for copy in p_in:
        copy.wait_recv()
    for p in range(3):
        columns = slice(OFF[p], OFF[p] + COLS[p])
        total = pj_s[:, columns]
        for a in range(4):
            for k in range(2):
                total = total + pr[p][a, k].astype(F32)
        out_ref[:, columns] = total
    for copy in sent:
        copy.wait_send()


def layer(queries, key_rows, values, out_weight, expert_ids, gate_ints, w_gate, w_up, w_down):
    count = queries.shape[0] // CHUNK
    blocks = [a.reshape(count, CHUNK, 128) for a in (queries, key_rows, values)]
    vm = pltpu.VMEM
    sem = lambda n: pltpu.SemaphoreType.DMA((n,))
    by = lambda *lead: [vm((*lead, n), BF) for n in COLS]
    scratch = [
        vm((count, CHUNK, 128), F32), vm((count, CHUNK, 128), F32), vm((count, CHUNK, 128), F32),
        vm((count, CHUNK, 128), F32), vm((128, 128), BF), vm((4, 128, 128), BF),
        vm((4, 2, 4, 64, 128), BF), vm((4, 2, 4, 64, 128), BF), vm((4, 2, 128, 2048), BF),
        vm((CB, 4, 64, CBW), BF), vm((CB, 4, 64, CBW), BF), vm((CB, 4, 64, CBW), F32), vm((64, 2048), F32),
        vm((64, 256), BF), vm((4, 2, 64, 256), BF), vm((4, 2, 64, 256), BF), vm((4, 2, 64, 256), BF),
        vm((3, 4, 256, 128), BF), vm((3, 4, 128, 256), BF),
        *by(4, 2, 64), *by(4, 16, 16), *by(4, 4, 4, 16), *by(4, 4, 4, 16), *by(4, 16, 16),
        *by(4, 2, 64), *by(4, 2, 64),
        vm((2048, 768), BF), vm((2048, 768), BF), vm((768, 2048), BF),
        sem(7), sem(4), sem(4), sem(8), sem(8), sem(4), sem(4), sem(4), sem(4), sem(16), sem(16),
        sem(24), sem(24), sem(24), sem(24), sem(48), sem(48), sem(48), sem(48), sem(24), sem(24),
    ]
    hbm = pl.BlockSpec(memory_space=pl.ANY)
    vmem = pl.BlockSpec(memory_space=pltpu.VMEM)
    return pl.pallas_call(
        body,
        out_shape=jax.ShapeDtypeStruct((64, 2048), F32),
        in_specs=[hbm, hbm, hbm, hbm, vmem, vmem, hbm, hbm, hbm],
        out_specs=vmem,
        scratch_shapes=scratch,
        compiler_params=pltpu.CompilerParams(
            collective_id=0, has_side_effects=True, vmem_limit_bytes=62 << 20
        ),
        cost_estimate=pl.CostEstimate(flops=13 * 10**9, bytes_accessed=14 * 10**6, transcendentals=10**6),
    )(*blocks, out_weight, expert_ids, gate_ints, w_gate[0], w_up[0], w_down[0])


def solution(mesh):
    placed = (
        P("seq", "head"),
        P("seq", "head"),
        P("seq", "head"),
        P("head", None),
        P(("seq", "head"), None),
        P(("seq", "head"), None),
        P(("seq", "head"), None, None),
        P(("seq", "head"), None, None),
        P(("seq", "head"), None, None),
    )
    return jax.shard_map(
        layer, mesh=mesh, in_specs=placed, out_specs=P(("seq", "head"), None), check_vma=False
    )
```

```python
import functools

import jax
import jax.numpy as jnp
from jax import lax
from jax.experimental import pallas as pl
from jax.experimental.pallas import tpu as pltpu
from jax.sharding import PartitionSpec as P

MESH = pl.DeviceIdType.MESH
BF = jnp.bfloat16
F32 = jnp.float32
COLS = (768, 640, 640)
OFF = (0, 768, 1408)
PLANE = ((1, 2), (0, 2), (0, 1))
ORDER = (5, 10, 15, 8, 2, 7, 13, 1, 4, 11, 14, 3, 12, 6, 9)
CB = 4
CBW = 512
HALF = 1024
STEPS = (0, 1, 2, 3)
CHUNK = 256


def partners():
    found = []
    for a in range(4):
        for b in range(4):
            for d in range(4):
                if 0 in (a, b, d) and (a, b, d) != (0, 0, 0):
                    found.append((a, b, d, 0))
    found.append((0, 0, 0, 1))
    for a in range(1, 4):
        found += [(a, 0, 0, 1), (0, a, 0, 1), (0, 0, a, 1)]
    return found


def body(
    q_h, k_h, v_h, w_h, ids_ref, gi_ref, wg_h, wu_h, wd_h, out_ref,
    q_s, k_s, v_s, o_s, st_s, st_r, at_s, ar0, ar1, w0, w1, rs_s, rs_r, pf_s, pj_s,
    vg_s, m0, m1, m2, sel_s, com_s, l0, l1, l2, ds0, ds1, ds2, r0, r1, r2,
    o0, o1, o2, rt0, rt1, rt2, pf0, pf1, pf2, px0, px1, px2, xr0, xr1, xr2,
    ps0, ps1, ps2, pr0, pr1, pr2, wg_s, wu_s, wd_s,
    loc_sem, st_ss, st_rs, at_ss, at_rs, w_ss, w_rs, wf_ss, wf_rs, rs_ss, rs_rs,
    m_ss, m_rs, l_ss, l_rs, d0_ss, d0_rs, d1_ss, d1_rs, d2_ss, d2_rs,
    e0_ss, e0_rs, e1_ss, e1_rs, e2_ss, e2_rs, x_ss, x_rs, p_ss, p_rs,
):
    meta, line = (m0, m1, m2), (l0, l1, l2)
    ds, rr, oo, rt = (ds0, ds1, ds2), (r0, r1, r2), (o0, o1, o2), (rt0, rt1, rt2)
    pf, px, xr, ps, pr = (pf0, pf1, pf2), (px0, px1, px2), (xr0, xr1, xr2), (ps0, ps1, ps2), (pr0, pr1, pr2)
    ar, ws = (ar0, ar1), (w0, w1)
    z = lax.axis_index("seq")
    head = lax.axis_index("head")
    y, x, c = head // 8, (head // 2) % 4, head % 2
    at = (x, y, z)
    other = 1 - c

    def dev(coords, core):
        return (coords[2], (coords[1] * 4 + coords[0]) * 2 + core)

    def moved(**shift):
        return tuple((at[i] + shift.get("xyz"[i], 0)) % 4 for i in range(3))

    def along(axis, d):
        return tuple((at[i] + d) % 4 if i == axis else at[i] for i in range(3))

    sent = []

    def remote(src, dst, ss, rs, device):
        return pltpu.make_async_remote_copy(
            src_ref=src, dst_ref=dst, send_sem=ss, recv_sem=rs, device_id=device, device_id_type=MESH
        )

    def send(*what):
        copy = remote(*what)
        copy.start()
        sent.append(copy)
        return copy

    loads = []
    for i, (src, dst) in enumerate(
        (
            (k_h, k_s), (v_h, v_s), (w_h.at[:, :HALF], w0.at[y, c]), (w_h.at[:, HALF:], w1.at[x, c]),
            (q_h, q_s), (wg_h, wg_s), (wu_h, wu_s), (wd_h, wd_s),
        )
    ):
        copy = pltpu.make_async_copy(src, dst, loc_sem.at[i])
        copy.start()
        loads.append(copy)

    barrier = pltpu.get_barrier_semaphore()
    greeted = partners()
    for dx, dy, dz, dc in greeted:
        core = other if dc else c
        pl.semaphore_signal(
            barrier, inc=1, device_id=dev(moved(x=dx, y=dy, z=dz), core), device_id_type=MESH
        )

    experts = lax.broadcasted_iota(jnp.int32, (64, 128), 1)
    named = jnp.zeros((64, 128), F32)
    gate = jnp.zeros((64, 128), F32)
    gates = gi_ref[...].astype(F32)
    gates = gates / jnp.sum(gates, axis=-1, keepdims=True)
    for k in range(8):
        hit = ids_ref[:, k : k + 1] == experts
        named = jnp.where(hit, 1.0, named)
        gate = jnp.where(hit, gates[:, k : k + 1], gate)
    before = (
        lax.broadcasted_iota(jnp.int32, (64, 64), 1) < lax.broadcasted_iota(jnp.int32, (64, 64), 0)
    ).astype(F32).astype(BF)
    rank = jnp.dot(before, named.astype(BF), preferred_element_type=F32)
    vg_s[:, :128] = jnp.where(named > 0.5, rank, -1.0).astype(BF)
    vg_s[:, 128:] = gate.astype(BF)

    loads[0].wait()
    loads[1].wait()
    count = q_s.shape[0]
    state = jnp.zeros((128, 128), F32)
    prefix = []
    for i in range(count):
        prefix.append(state)
        state = state + lax.dot_general(
            k_s[i].astype(BF), v_s[i].astype(BF), (((0,), (0,)), ((), ())), preferred_element_type=F32
        )
    st_s[...] = state.astype(BF)
    loads[2].wait()
    loads[3].wait()

    pl.semaphore_wait(barrier, len(greeted))

    st_in = [
        send(st_s, st_r.at[z], st_ss.at[d], st_rs.at[d], dev(along(2, d), c)) for d in (1, 2, 3)
    ]
    w_in, wf_in = {}, []
    lines = (1, 0)
    for d in (2, 1, 3):
        for v in range(2):
            mine = ws[v].at[at[lines[v]], c]
            w_in[v, d] = send(mine, mine, w_ss.at[v * 4 + d], w_rs.at[v * 4 + d], dev(along(lines[v], d), c))
    for v in range(2):
        mine = ws[v].at[at[lines[v]], c]
        wf_in.append(send(mine, mine, wf_ss.at[v * 4], wf_rs.at[v * 4], dev(at, other)))
    meta_in = []
    for p in range(3):
        meta[p][at[p], c] = vg_s[...]
        for i in range(1, 8):
            d, k = i // 2, i % 2
            meta_in.append(
                send(
                    vg_s, meta[p].at[at[p], c], m_ss.at[p * 8 + i], m_rs.at[p * 8 + i],
                    dev(along(p, d), other if k else c),
                )
            )

    loads[4].wait()
    lower = lax.broadcasted_iota(jnp.int32, (CHUNK, CHUNK), 1) <= lax.broadcasted_iota(
        jnp.int32, (CHUNK, CHUNK), 0
    )
    for i in range(count):
        qb, kb = q_s[i].astype(BF), k_s[i].astype(BF)
        scores = lax.dot_general(qb, kb, (((1,), (1,)), ((), ())), preferred_element_type=F32)
        scores = jnp.where(lower, scores, 0.0).astype(BF)
        o_s[i] = jnp.dot(scores, v_s[i].astype(BF), preferred_element_type=F32)
    for copy in st_in:
        copy.wait_recv()
    earlier = jnp.zeros((128, 128), F32)
    for d in (1, 2, 3):
        source = (z - d + 4) % 4
        earlier = earlier + jnp.where(source < z, st_r[source].astype(F32), 0.0)
    for i in range(count):
        total = (prefix[i] + earlier).astype(BF)
        mixed = o_s[i] + jnp.dot(q_s[i].astype(BF), total, preferred_element_type=F32)
        mixed = mixed * lax.rsqrt(jnp.mean(mixed * mixed, axis=-1, keepdims=True) + 1e-06)
        mixed = mixed.astype(BF)
        for j in range(2):
            for k in range(2):
                at_s[i // 2, k, (i % 2) * 2 + j] = mixed[(2 * j + k) * 64 : (2 * j + k + 1) * 64]
    at_in = []
    for i in (4, 5, 2, 3, 6, 7, 1):
        d, k = i // 2, i % 2
        core = other if k else c
        for v in range(2):
            to = (at[lines[v]] + d) % 4
            src = at_s.at[to, core] if v == 0 else at_s.at[:, core, to]
            at_in.append(
                send(
                    src, ar[v].at[at[lines[v]], c], at_ss.at[v * 8 + i], at_rs.at[v * 8 + i],
                    dev(along(lines[v], d), core),
                )
            )
    ar0[y, c] = at_s[y, c]
    ar1[x, c] = at_s[:, c, x]

    for copy in meta_in:
        copy.wait_recv()
    row_e = lax.broadcasted_iota(jnp.int32, (128, 256), 0)
    col_r = lax.broadcasted_iota(jnp.int32, (128, 256), 1)
    first, second = col_r // 64, (col_r // 16) % 4
    same = (row_e // 64) == ((col_r // 8) % 2)
    slot = jnp.where(same, (col_r % 8).astype(F32), -2.0)
    for p in range(3):
        if p == 0:
            expert = second * 32 + first * 8 + x * 2 + c
        elif p == 1:
            expert = second * 32 + y * 8 + first * 2 + c
        else:
            expert = z * 32 + second * 8 + first * 2 + c
        spread = (row_e == expert).astype(F32).astype(BF)

        def make(a, carry, p=p, spread=spread):
            both = meta[p][a].reshape(128, 256)
            ranks = jnp.dot(both[:, :128], spread, preferred_element_type=F32)
            weight = jnp.dot(both[:, 128:], spread, preferred_element_type=F32)
            hit = ranks == slot
            com_s[p, a] = jnp.where(hit, weight, 0.0).astype(BF)
            sel_s[p, a] = jnp.where(hit, 1.0, 0.0).T.astype(BF)
            return carry

        lax.fori_loop(0, 4, make, 0)

    for d in (1, 3, 2):
        for v in range(2):
            w_in[v, d].wait_recv()
            got = ws[v].at[(at[lines[v]] - d + 4) % 4, c]
            wf_in.append(send(got, got, wf_ss.at[v * 4 + d], wf_rs.at[v * 4 + d], dev(at, other)))
    for copy in at_in:
        copy.wait_recv()
    for copy in wf_in:
        copy.wait_recv()
    lhs = [
        jnp.concatenate([ar[v][i // 2, i % 2].reshape(256, 128) for i in range(8)], axis=1)
        for v in range(2)
    ]
    rs_in = []
    for b in range(CB):
        v, low = b % 2, (b // 2) * CBW
        part = jnp.dot(
            lhs[v], ws[v][:, :, :, low : low + CBW].reshape(1024, CBW), preferred_element_type=F32
        ).reshape(4, 64, CBW)
        pf_s[b] = part
        rs_s[b] = part.astype(BF)
        for d in (2, 1, 3):
            i = b * 4 + d
            rs_in.append(
                send(
                    rs_s.at[b, (at[v] + d) % 4], rs_r.at[b, at[v]], rs_ss.at[i], rs_rs.at[i],
                    dev(along(v, d), c),
                )
            )
    for copy in rs_in:
        copy.wait_recv()
    square = jnp.zeros((64, 1), F32)
    for b in range(CB):
        v, low = b % 2, (b % 2) * HALF + (b // 2) * CBW
        total = pf_s[b, at[v]]
        for d in (1, 2, 3):
            total = total + rs_r[b, (at[v] - d + 4) % 4].astype(F32)
        pj_s[:, low : low + CBW] = total
        square = square + jnp.sum(total * total, axis=-1, keepdims=True)
    scale = lax.rsqrt(square / 2048.0 + 1e-06)

    line_in = {}
    for p in range(3):
        line[p][at[p], c] = (pj_s[:, OFF[p] : OFF[p] + COLS[p]] * scale).astype(BF)

    def pass_on(p, d):
        block = line[p].at[(at[p] - d + 4) % 4, c]
        i = p * 8 + d * 2 + 1
        line_in[p, d * 2 + 1] = send(block, block, l_ss.at[i], l_rs.at[i], dev(at, other))

    for d in (2, 1, 3):
        for p in (1, 2, 0):
            own = line[p].at[at[p], c]
            i = p * 8 + d * 2
            line_in[p, d * 2] = send(own, own, l_ss.at[i], l_rs.at[i], dev(along(p, d), c))
    for p in (1, 2, 0):
        pass_on(p, 0)
    for d in (1, 3, 2):
        for p in (1, 2, 0):
            line_in[p, d * 2].wait_recv()
            pass_on(p, d)

    here = [at[PLANE[p][0]] * 4 + at[PLANE[p][1]] for p in range(3)]

    def pick(p, d):
        source = (at[p] - d + 4) % 4
        line_in[p, d * 2 + 1].wait_recv()
        picked = jnp.dot(
            sel_s[p, source], line[p][source].reshape(128, COLS[p]), preferred_element_type=F32
        )
        ds[p][source] = picked.astype(BF).reshape(16, 16, COLS[p])

    def out0(i, k):
        a, first, second = (x + i) % 4, (y + k // 4) % 4, (z + k % 4) % 4
        j = i * 16 + k
        return ds0.at[a, first * 4 + second], r0.at[a, y, z], d0_ss.at[j], d0_rs.at[j], dev((x, first, second), c)

    def out1(i, b):
        first, second = (x + 4 - i) % 4, (z + b) % 4
        j = i * 4 + b
        return ds1.at[:, first * 4 + second], r1.at[x, :, z], d1_ss.at[j], d1_rs.at[j], dev((first, y, second), c)

    def out2(i, b):
        first, second = (x + 4 - i) % 4, (y + b) % 4
        j = i * 4 + b
        return ds2.at[:, first * 4 + second], r2.at[x, y], d2_ss.at[j], d2_rs.at[j], dev((first, second, z), c)

    def back0(i, k):
        a, first, second = (x + i) % 4, (y + k // 4) % 4, (z + k % 4) % 4
        j = i * 16 + k
        return o0.at[a, first, second], rt0.at[a, y * 4 + z], e0_ss.at[j], e0_rs.at[j], dev((x, first, second), c)

    def back1(i, b):
        first, second = (x + i) % 4, (z + b) % 4
        j = i * 4 + b
        return o1.at[first, :, second], rt1.at[:, x * 4 + z], e1_ss.at[j], e1_rs.at[j], dev((first, y, second), c)

    def back2(i, b):
        first, second = (x + i) % 4, (y + b) % 4
        j = i * 4 + b
        return o2.at[first, second], rt2.at[:, x * 4 + y], e2_ss.at[j], e2_rs.at[j], dev((first, second, z), c)

    for d in (0, 1, 3, 2):
        for p in (1, 2):
            pick(p, d)
    r1[x, :, z] = ds1[:, here[1]]
    r2[x, y] = ds2[:, here[2]]
    for i in STEPS:
        pick(0, (4 - i) % 4)
        a = (x + i) % 4
        r0[a, y, z] = ds0[a, here[0]]
        for b in (2, 1, 3, 0):
            if (i, b) != (0, 0):
                send(*out1(i, b))
                send(*out2(i, b))
            for k in ORDER[b * 4 : b * 4 + 4]:
                send(*out0(i, k))
    for copy in loads[5:]:
        copy.wait()

    def expert_rows(turn, carry):
        step = (turn + STEPS[0]) % 4
        block = (x + step) % 4
        for k in range(1, 16):
            remote(*out0(step, k)).wait_recv()
        for b in range(1, 4):
            remote(*out1(step, b)).wait_recv()
            remote(*out2(step, b)).wait_recv()

        @pl.when(step != 0)
        def _():
            remote(*out1(step, 0)).wait_recv()
            remote(*out2(step, 0)).wait_recv()

        rows = [rr[p][block].reshape(256, COLS[p]) for p in range(3)]
        gate_val = jnp.zeros((256, 768), F32)
        up_val = jnp.zeros((256, 768), F32)
        for p in range(3):
            gate_val = gate_val + jnp.dot(
                rows[p], wg_s[OFF[p] : OFF[p] + COLS[p]], preferred_element_type=F32
            )
            up_val = up_val + jnp.dot(
                rows[p], wu_s[OFF[p] : OFF[p] + COLS[p]], preferred_element_type=F32
            )
        act = (gate_val / (1.0 + jnp.exp(-gate_val)) * up_val).astype(BF)
        for p in range(3):
            result = jnp.dot(act, wd_s[:, OFF[p] : OFF[p] + COLS[p]], preferred_element_type=F32)
            oo[p][block] = result.astype(BF).reshape(4, 4, 16, COLS[p])
        rt0[block, here[0]] = o0[block, y, z]
        for b in (2, 1, 3):
            remote(*back1(step, b)).start()
            remote(*back2(step, b)).start()
            for k in ORDER[b * 4 : b * 4 + 4]:
                remote(*back0(step, k)).start()
        for k in ORDER[:4]:
            remote(*back0(step, k)).start()

        @pl.when(step != 0)
        def _():
            remote(*back1(step, 0)).start()
            remote(*back2(step, 0)).start()

        @pl.when(step == 0)
        def _():
            rt1[:, here[1]] = o1[x, :, z]
            rt2[:, here[2]] = o2[x, y]

        return carry

    lax.fori_loop(0, 4, expert_rows, 0)

    x_in, p_in = {}, []

    def combine(p, d):
        to = (at[p] + d) % 4
        sums = jnp.dot(
            com_s[p, to], rt[p][to].reshape(256, COLS[p]), preferred_element_type=F32
        ).reshape(2, 64, COLS[p])
        pf[p][d] = jnp.where(c == 0, sums[0], sums[1])
        px[p][d] = jnp.where(c == 0, sums[1], sums[0]).astype(BF)
        i = p * 4 + d
        x_in[p, d] = send(px[p].at[d], xr[p].at[d], x_ss.at[i], x_rs.at[i], dev(at, other))

    def give(p, d):
        x_in[p, d].wait_recv()
        total = pf[p][d] + xr[p][d].astype(F32)
        if d == 0:
            pf[p][d] = total
            return
        ps[p][d] = total.astype(BF)
        i = p * 4 + d
        p_in.append(send(ps[p].at[d], pr[p].at[d], p_ss.at[i], p_rs.at[i], dev(along(p, d), c)))

    for i in STEPS:
        for k in range(1, 16):
            remote(*back0(i, k)).wait_recv()
        combine(0, i)
    for i in range(4):
        for b in range(4):
            if (i, b) != (0, 0):
                remote(*back1(i, b)).wait_recv()
                remote(*back2(i, b)).wait_recv()
    for d in STEPS:
        give(0, d)
    for d in (2, 1, 3, 0):
        for p in (1, 2):
            combine(p, d)
    for d in (2, 1, 3, 0):
        for p in (1, 2):
            give(p, d)
    for copy in p_in:
        copy.wait_recv()
    for p in range(3):
        columns = slice(OFF[p], OFF[p] + COLS[p])
        total = pj_s[:, columns] + pf[p][0]
        for d in range(1, 4):
            total = total + pr[p][d].astype(F32)
        out_ref[:, columns] = total
    for copy in sent:
        copy.wait_send()
    for i in range(4):
        for k in range(1, 16):
            remote(*back0(i, k)).wait_send()
        for b in range(4):
            if (i, b) != (0, 0):
                remote(*back1(i, b)).wait_send()
                remote(*back2(i, b)).wait_send()


def layer(queries, key_rows, values, out_weight, expert_ids, gate_ints, w_gate, w_up, w_down):
    count = queries.shape[0] // CHUNK
    blocks = [a.reshape(count, CHUNK, 128) for a in (queries, key_rows, values)]
    vm = pltpu.VMEM
    sem = lambda n: pltpu.SemaphoreType.DMA((n,))
    by = lambda *lead: [vm((*lead, n), BF) for n in COLS]
    scratch = [
        vm((count, CHUNK, 128), F32), vm((count, CHUNK, 128), F32), vm((count, CHUNK, 128), F32),
        vm((count, CHUNK, 128), F32), vm((128, 128), BF), vm((4, 128, 128), BF),
        vm((4, 2, 4, 64, 128), BF), vm((4, 2, 4, 64, 128), BF), vm((4, 2, 4, 64, 128), BF),
        vm((4, 2, 128, HALF), BF), vm((4, 2, 128, HALF), BF),
        vm((CB, 4, 64, CBW), BF), vm((CB, 4, 64, CBW), BF), vm((CB, 4, 64, CBW), F32), vm((64, 2048), F32),
        vm((64, 256), BF), vm((4, 2, 64, 256), BF), vm((4, 2, 64, 256), BF), vm((4, 2, 64, 256), BF),
        vm((3, 4, 256, 128), BF), vm((3, 4, 128, 256), BF),
        *by(4, 2, 64), *by(4, 16, 16), *by(4, 4, 4, 16), *by(4, 4, 4, 16), *by(4, 16, 16),
        *[vm((4, 64, n), F32) for n in COLS], *by(4, 64), *by(4, 64), *by(4, 64), *by(4, 64),
        vm((2048, 768), BF), vm((2048, 768), BF), vm((768, 2048), BF),
        sem(8), sem(4), sem(4), sem(16), sem(16), sem(8), sem(8), sem(8), sem(8), sem(16), sem(16),
        sem(24), sem(24), sem(24), sem(24), sem(64), sem(64), sem(16), sem(16), sem(16), sem(16),
        sem(64), sem(64), sem(16), sem(16), sem(16), sem(16), sem(12), sem(12), sem(12), sem(12),
    ]
    hbm = pl.BlockSpec(memory_space=pl.ANY)
    vmem = pl.BlockSpec(memory_space=pltpu.VMEM)
    return pl.pallas_call(
        body,
        out_shape=jax.ShapeDtypeStruct((64, 2048), F32),
        in_specs=[hbm, hbm, hbm, hbm, vmem, vmem, hbm, hbm, hbm],
        out_specs=vmem,
        scratch_shapes=scratch,
        compiler_params=pltpu.CompilerParams(
            collective_id=0, has_side_effects=True, vmem_limit_bytes=62 << 20
        ),
        cost_estimate=pl.CostEstimate(flops=13 * 10**9, bytes_accessed=14 * 10**6, transcendentals=10**6),
    )(*blocks, out_weight, expert_ids, gate_ints, w_gate[0], w_up[0], w_down[0])


def solution(mesh):
    placed = (
        P("seq", "head"),
        P("seq", "head"),
        P("seq", "head"),
        P("head", None),
        P(("seq", "head"), None),
        P(("seq", "head"), None),
        P(("seq", "head"), None, None),
        P(("seq", "head"), None, None),
        P(("seq", "head"), None, None),
    )
    return jax.shard_map(
        layer, mesh=mesh, in_specs=placed, out_specs=P(("seq", "head"), None), check_vma=False
    )
```

```python
import functools

import jax
import jax.numpy as jnp
from jax import lax
from jax.experimental import pallas as pl
from jax.experimental.pallas import tpu as pltpu
from jax.sharding import PartitionSpec as P

MESH = pl.DeviceIdType.MESH
BF = jnp.bfloat16
F32 = jnp.float32
COLS = (768, 640, 640)
OFF = (0, 768, 1408)
PLANE = ((1, 2), (0, 2), (0, 1))
ORDER = (5, 10, 15, 8, 2, 7, 13, 1, 4, 11, 14, 3, 12, 6, 9)
CB = 4
CBW = 512
HALF = 1024
STEPS = (1, 2, 3, 0)
CHUNK = 256


def partners():
    found = []
    for a in range(4):
        for b in range(4):
            for d in range(4):
                if 0 in (a, b, d) and (a, b, d) != (0, 0, 0):
                    found.append((a, b, d, 0))
    found.append((0, 0, 0, 1))
    for a in range(1, 4):
        found += [(a, 0, 0, 1), (0, a, 0, 1), (0, 0, a, 1)]
    return found


def body(
    q_h, k_h, v_h, w_h, ids_ref, gi_ref, wg_h, wu_h, wd_h, out_ref,
    q_s, k_s, v_s, o_s, st_s, st_r, at_s, ar0, ar1, w0, w1, rs_s, rs_r, pf_s, pj_s,
    vg_s, m0, m1, m2, sel_s, com_s, l0, l1, l2, ds0, ds1, ds2, r0, r1, r2,
    o0, o1, o2, rt0, rt1, rt2, pf0, pf1, pf2, px0, px1, px2, xr0, xr1, xr2,
    ps0, ps1, ps2, pr0, pr1, pr2, wg_s, wu_s, wd_s,
    loc_sem, st_ss, st_rs, at_ss, at_rs, w_ss, w_rs, wf_ss, wf_rs, rs_ss, rs_rs,
    m_ss, m_rs, l_ss, l_rs, d_ss, d_rs, e_ss, e_rs, x_ss, x_rs, p_ss, p_rs, q_ss, q_rs, z_ss, z_rs,
):
    meta, line = (m0, m1, m2), (l0, l1, l2)
    ds, rr, oo, rt = (ds0, ds1, ds2), (r0, r1, r2), (o0, o1, o2), (rt0, rt1, rt2)
    pf, px, xr, ps, pr = (pf0, pf1, pf2), (px0, px1, px2), (xr0, xr1, xr2), (ps0, ps1, ps2), (pr0, pr1, pr2)
    ar, ws = (ar0, ar1), (w0, w1)
    z = lax.axis_index("seq")
    head = lax.axis_index("head")
    y, x, c = head // 8, (head // 2) % 4, head % 2
    at = (x, y, z)
    other = 1 - c

    def dev(coords, core):
        return (coords[2], (coords[1] * 4 + coords[0]) * 2 + core)

    def moved(**shift):
        return tuple((at[i] + shift.get("xyz"[i], 0)) % 4 for i in range(3))

    def along(axis, d):
        return tuple((at[i] + d) % 4 if i == axis else at[i] for i in range(3))

    sent = []

    def remote(src, dst, ss, rs, device):
        return pltpu.make_async_remote_copy(
            src_ref=src, dst_ref=dst, send_sem=ss, recv_sem=rs, device_id=device, device_id_type=MESH
        )

    def send(*what):
        copy = remote(*what)
        copy.start()
        sent.append(copy)
        return copy

    loads = []
    for i, (src, dst) in enumerate(
        (
            (k_h, k_s), (v_h, v_s), (w_h.at[:, :HALF], w0.at[y, c]), (w_h.at[:, HALF:], w1.at[x, c]),
            (q_h, q_s), (wg_h, wg_s), (wu_h, wu_s), (wd_h, wd_s),
        )
    ):
        copy = pltpu.make_async_copy(src, dst, loc_sem.at[i])
        copy.start()
        loads.append(copy)

    barrier = pltpu.get_barrier_semaphore()
    greeted = partners()
    for dx, dy, dz, dc in greeted:
        core = other if dc else c
        pl.semaphore_signal(
            barrier, inc=1, device_id=dev(moved(x=dx, y=dy, z=dz), core), device_id_type=MESH
        )

    ids = ids_ref[...]
    experts = lax.broadcasted_iota(jnp.int32, (128, 64), 0)
    gates = gi_ref[...].astype(F32)
    gates = gates / jnp.sum(gates, axis=0, keepdims=True)
    named = jnp.zeros((128, 64), F32)
    for k in range(8):
        named = jnp.where(ids[k : k + 1] == experts, 1.0, named)
    before = (
        lax.broadcasted_iota(jnp.int32, (64, 64), 0) < lax.broadcasted_iota(jnp.int32, (64, 64), 1)
    ).astype(F32).astype(BF)
    rank = jnp.dot(named.astype(BF), before, preferred_element_type=F32)
    ranks = jnp.concatenate(
        [
            jnp.sum(jnp.where(ids[k : k + 1] == experts, rank, 0.0), axis=0, keepdims=True)
            for k in range(8)
        ],
        axis=0,
    )
    upper = jnp.concatenate([ids.astype(F32), gates], axis=1)
    under = jnp.concatenate([ranks, ranks], axis=1)
    vg_s[...] = jnp.concatenate([upper, under], axis=0).astype(BF)

    loads[0].wait()
    loads[1].wait()
    count = q_s.shape[0]
    state = jnp.zeros((128, 128), F32)
    prefix = []
    for i in range(count):
        prefix.append(state)
        state = state + lax.dot_general(
            k_s[i].astype(BF), v_s[i].astype(BF), (((0,), (0,)), ((), ())), preferred_element_type=F32
        )
    st_s[...] = state.astype(BF)
    loads[2].wait()
    loads[3].wait()

    pl.semaphore_wait(barrier, len(greeted))

    st_in = [
        send(st_s, st_r.at[z], st_ss.at[d], st_rs.at[d], dev(along(2, d), c)) for d in (1, 2, 3)
    ]
    lines = (1, 0)

    def straight(v, a):
        return ws[v].at[a, c, :, :CBW]

    def quarter(v, a):
        return ws[v].at[a, c, :, pl.ds(pl.multiple_of(CBW + 128 * z, 128), 128)]

    w_in, q_in, wf_in = {}, {}, {}
    for d in (2, 1, 3):
        for v in range(2):
            i = v * 4 + d
            mine = quarter(v, at[lines[v]])
            q_in[v, d] = send(mine, mine, q_ss.at[i], q_rs.at[i], dev(along(lines[v], d), c))
    for d in (2, 1, 3):
        for v in range(2):
            i = v * 4 + d
            mine = straight(v, at[lines[v]])
            w_in[v, d] = send(mine, mine, w_ss.at[i], w_rs.at[i], dev(along(lines[v], d), c))

    def hand_on(v, d, half):
        got = ws[v].at[(at[lines[v]] - d + 4) % 4, c, :, half * CBW : (half + 1) * CBW]
        i = half * 8 + v * 4 + d
        wf_in[v, d, half] = send(got, got, wf_ss.at[i], wf_rs.at[i], dev(at, other))

    for v in range(2):
        for half in range(2):
            hand_on(v, 0, half)
    meta_in = []
    for p in range(3):
        meta[p][0, c] = vg_s[...]
        for i in range(1, 8):
            d, k = i // 2, i % 2
            meta_in.append(
                send(
                    vg_s, meta[p].at[(4 - d) % 4, c], m_ss.at[p * 8 + i], m_rs.at[p * 8 + i],
                    dev(along(p, d), other if k else c),
                )
            )

    loads[4].wait()
    lower = lax.broadcasted_iota(jnp.int32, (CHUNK, CHUNK), 1) <= lax.broadcasted_iota(
        jnp.int32, (CHUNK, CHUNK), 0
    )
    for i in range(count):
        qb, kb = q_s[i].astype(BF), k_s[i].astype(BF)
        scores = lax.dot_general(qb, kb, (((1,), (1,)), ((), ())), preferred_element_type=F32)
        scores = jnp.where(lower, scores, 0.0).astype(BF)
        o_s[i] = jnp.dot(scores, v_s[i].astype(BF), preferred_element_type=F32)
    z_in = {}
    for d in (1, 3, 2):
        for v in range(2):
            q_in[v, d].wait_recv()
            got = quarter(v, (at[lines[v]] - d + 4) % 4)
            for e in (2, 1, 3):
                i = v * 16 + d * 4 + e
                z_in[v, d, e] = send(got, got, z_ss.at[i], z_rs.at[i], dev(along(2, e), c))
    for copy in st_in:
        copy.wait_recv()
    earlier = jnp.zeros((128, 128), F32)
    for d in (1, 2, 3):
        source = (z - d + 4) % 4
        earlier = earlier + jnp.where(source < z, st_r[source].astype(F32), 0.0)
    for i in range(count):
        total = (prefix[i] + earlier).astype(BF)
        mixed = o_s[i] + jnp.dot(q_s[i].astype(BF), total, preferred_element_type=F32)
        mixed = mixed * lax.rsqrt(jnp.mean(mixed * mixed, axis=-1, keepdims=True) + 1e-06)
        mixed = mixed.astype(BF)
        for j in range(2):
            for k in range(2):
                at_s[i // 2, k, (i % 2) * 2 + j] = mixed[(2 * j + k) * 64 : (2 * j + k + 1) * 64]
    at_in = []
    for i in (4, 5, 2, 3, 6, 7, 1):
        d, k = i // 2, i % 2
        core = other if k else c
        for v in range(2):
            to = (at[lines[v]] + d) % 4
            src = at_s.at[to, core] if v == 0 else at_s.at[:, core, to]
            at_in.append(
                send(
                    src, ar[v].at[at[lines[v]], c], at_ss.at[v * 8 + i], at_rs.at[v * 8 + i],
                    dev(along(lines[v], d), core),
                )
            )
    ar0[y, c] = at_s[y, c]
    ar1[x, c] = at_s[:, c, x]

    for copy in meta_in:
        copy.wait_recv()
    row_r = lax.broadcasted_iota(jnp.int32, (256, 128), 0)
    base = lax.broadcasted_iota(jnp.int32, (8, 128), 1) // 64 * 1024
    first, second = row_r // 64, (row_r // 16) % 4
    for p in range(3):
        one, two = (first + at[PLANE[p][0]]) % 4, (second + at[PLANE[p][1]]) % 4
        if p == 0:
            expert = two * 32 + one * 8 + x * 2 + c
        elif p == 1:
            expert = two * 32 + y * 8 + one * 2 + c
        else:
            expert = z * 32 + two * 8 + one * 2 + c
        wanted = (row_r // 8) % 2 * 1024 + expert * 8 + row_r % 8

        def make(d, carry, p=p, wanted=wanted):
            both = meta[p][d].astype(F32)
            code = jnp.concatenate([both[0, :8, :64], both[1, :8, :64]], axis=1) * 8.0
            code = code + jnp.concatenate([both[0, 8:, :64], both[1, 8:, :64]], axis=1)
            code = code.astype(jnp.int32) + base
            weight = jnp.concatenate([both[0, :8, 64:], both[1, :8, 64:]], axis=1)
            sel = jnp.zeros((256, 128), F32)
            com = jnp.zeros((256, 128), F32)
            for k in range(8):
                hit = code[k : k + 1] == wanted
                sel = jnp.where(hit, 1.0, sel)
                com = jnp.where(hit, weight[k : k + 1], com)
            sel_s[p, d] = sel.astype(BF)
            com_s[p, d] = com.T.astype(BF)
            return carry

        lax.fori_loop(0, 4, make, 0)

    for d in (1, 3, 2):
        for v in range(2):
            w_in[v, d].wait_recv()
            hand_on(v, d, 0)
    for d in (1, 3, 2):
        for v in range(2):
            for e in (1, 2, 3):
                z_in[v, d, e].wait_recv()
            hand_on(v, d, 1)
    for copy in at_in:
        copy.wait_recv()
    lhs = [
        jnp.concatenate([ar[v][i // 2, i % 2].reshape(256, 128) for i in range(8)], axis=1)
        for v in range(2)
    ]
    rs_in = []
    for b in range(CB):
        v, low = b % 2, (b // 2) * CBW
        for d in range(4):
            wf_in[v, d, b // 2].wait_recv()
        part = jnp.dot(
            lhs[v], ws[v][:, :, :, low : low + CBW].reshape(1024, CBW), preferred_element_type=F32
        ).reshape(4, 64, CBW)
        pf_s[b] = part
        rs_s[b] = part.astype(BF)
        for d in (2, 1, 3):
            i = b * 4 + d
            rs_in.append(
                send(
                    rs_s.at[b, (at[v] + d) % 4], rs_r.at[b, at[v]], rs_ss.at[i], rs_rs.at[i],
                    dev(along(v, d), c),
                )
            )
    for copy in rs_in:
        copy.wait_recv()
    square = jnp.zeros((64, 1), F32)
    for b in range(CB):
        v, low = b % 2, (b % 2) * HALF + (b // 2) * CBW
        total = pf_s[b, at[v]]
        for d in (1, 2, 3):
            total = total + rs_r[b, (at[v] - d + 4) % 4].astype(F32)
        pj_s[:, low : low + CBW] = total
        square = square + jnp.sum(total * total, axis=-1, keepdims=True)
    scale = lax.rsqrt(square / 2048.0 + 1e-06)

    line_in = {}
    for p in range(3):
        line[p][0, c] = (pj_s[:, OFF[p] : OFF[p] + COLS[p]] * scale).astype(BF)

    def pass_on(p, d):
        block = line[p].at[(4 - d) % 4, c]
        i = p * 8 + d * 2 + 1
        line_in[p, d * 2 + 1] = send(block, block, l_ss.at[i], l_rs.at[i], dev(at, other))

    for p in (1, 2, 0):
        pass_on(p, 0)
    for d in (2, 1, 3):
        for p in (1, 2, 0):
            own = line[p].at[0, c]
            i = p * 8 + d * 2
            line_in[p, d * 2] = send(
                own, line[p].at[4 - d, c], l_ss.at[i], l_rs.at[i], dev(along(p, d), c)
            )

    def pick(p, rel):
        line_in[p, (4 - rel) % 4 * 2 + 1].wait_recv()
        picked = jnp.dot(
            sel_s[p, rel], line[p][rel].reshape(128, COLS[p]), preferred_element_type=F32
        )
        ds[p][rel] = picked.astype(BF).reshape(16, 16, COLS[p])

    def minus(k):
        return (4 - k // 4) % 4 * 4 + (4 - k % 4) % 4

    def plane_dev(p, k):
        coords = [None] * 3
        coords[p] = at[p]
        coords[PLANE[p][0]] = (at[PLANE[p][0]] + k // 4) % 4
        coords[PLANE[p][1]] = (at[PLANE[p][1]] + k % 4) % 4
        return dev(coords, c)

    def rows(ref, p, part, first, second):
        if p == 0:
            return ref.at[part, first, second]
        which = 0 if part == 0 else slice(1, 4)
        return ref.at[first, which, second] if p == 1 else ref.at[first, second, which]

    def blocks(ref, p, part, k):
        if p == 0 or part == 0:
            return ref.at[part, k]
        return ref.at[1:4, k]

    def out(p, part, k):
        j = part * 16 + k
        n = minus(k)
        return (
            blocks(ds[p], p, part, k), rows(rr[p], p, part, n // 4, n % 4), d_ss.at[p * 64 + j],
            d_rs.at[p * 64 + j], plane_dev(p, k),
        )

    def back(p, part, k):
        j = part * 16 + k
        return (
            rows(oo[p], p, part, k // 4, k % 4), blocks(rt[p], p, part, minus(k)), e_ss.at[p * 64 + j],
            e_rs.at[p * 64 + j], plane_dev(p, k),
        )

    d_in, e_in = {}, {}

    def go(p, part, k):
        d_in[p, part, k] = send(*out(p, part, k))

    for p in (1, 2, 0):
        pick(p, 0)
        for k in ORDER:
            go(p, 0, k)
    for p in range(3):
        if p == 0:
            r0[0, 0, 0] = ds0[0, 0]
        elif p == 1:
            r1[0, 0, 0] = ds1[0, 0]
        else:
            r2[0, 0, 0] = ds2[0, 0]
    for d in (1, 3, 2):
        for p in (1, 2, 0):
            line_in[p, d * 2].wait_recv()
            pass_on(p, d)
    for rel in (3, 1, 2):
        for p in (1, 2):
            pick(p, rel)
    r1[0, 1:4, 0] = ds1[1:4, 0]
    r2[0, 0, 1:4] = ds2[1:4, 0]
    for i in STEPS:
        if i:
            pick(0, i)
            r0[i, 0, 0] = ds0[i, 0]
        for b in (2, 1, 3, 0):
            k = (4 - i) % 4 * 4 + b
            if k:
                go(1, 1, k)
                go(2, 1, k)
            if i:
                for k in ORDER[b * 4 : b * 4 + 4]:
                    go(0, i, k)
    for copy in loads[5:]:
        copy.wait()

    def expert_rows(i):
        taken = [rr[p][i].reshape(256, COLS[p]) for p in range(3)]
        gate_val = jnp.zeros((256, 768), F32)
        up_val = jnp.zeros((256, 768), F32)
        for p in range(3):
            gate_val = gate_val + jnp.dot(
                taken[p], wg_s[OFF[p] : OFF[p] + COLS[p]], preferred_element_type=F32
            )
            up_val = up_val + jnp.dot(
                taken[p], wu_s[OFF[p] : OFF[p] + COLS[p]], preferred_element_type=F32
            )
        act = (gate_val / (1.0 + jnp.exp(-gate_val)) * up_val).astype(BF)
        for p in range(3):
            result = jnp.dot(act, wd_s[:, OFF[p] : OFF[p] + COLS[p]], preferred_element_type=F32)
            oo[p][i] = result.astype(BF).reshape(4, 4, 16, COLS[p])

    def come(p, part, k):
        e_in[p, part, k] = send(*back(p, part, k))

    for i in STEPS:
        for k in range(1, 16):
            d_in[0, i, k].wait_recv()
        for b in range(4):
            k = (4 - i) % 4 * 4 + b
            if k:
                for p in (1, 2):
                    d_in[p, 0, k].wait_recv()
                    d_in[p, 1, k].wait_recv()
        expert_rows(i)
        rt0[i, 0] = o0[i, 0, 0]
        for b in (2, 1, 3, 0):
            k = i * 4 + b
            if k:
                come(1, 1, k)
                come(2, 1, k)
            for k in ORDER[b * 4 : b * 4 + 4]:
                come(0, i, k)
    for k in ORDER:
        for p in (1, 2):
            come(p, 0, k)
    rt1[:, 0] = o1[0, :, 0]
    rt2[:, 0] = o2[0, 0]

    x_in, p_in = {}, []

    def combine(p, d):
        sums = jnp.dot(
            com_s[p, d], rt[p][d].reshape(256, COLS[p]), preferred_element_type=F32
        ).reshape(2, 64, COLS[p])
        pf[p][d] = jnp.where(c == 0, sums[0], sums[1])
        px[p][d] = jnp.where(c == 0, sums[1], sums[0]).astype(BF)
        i = p * 4 + d
        x_in[p, d] = send(px[p].at[d], xr[p].at[d], x_ss.at[i], x_rs.at[i], dev(at, other))

    def give(p, d):
        x_in[p, d].wait_recv()
        total = pf[p][d] + xr[p][d].astype(F32)
        if d == 0:
            pf[p][d] = total
            return
        ps[p][d] = total.astype(BF)
        i = p * 4 + d
        p_in.append(send(ps[p].at[d], pr[p].at[d], p_ss.at[i], p_rs.at[i], dev(along(p, d), c)))

    for i in STEPS[:3]:
        for k in range(1, 16):
            e_in[0, i, k].wait_recv()
        combine(0, i)
    for d in STEPS[:3]:
        give(0, d)
    for k in range(1, 16):
        for p in (1, 2):
            e_in[p, 1, k].wait_recv()
    for d in (2, 1, 3):
        for p in (1, 2):
            combine(p, d)
    for d in (2, 1, 3):
        for p in (1, 2):
            give(p, d)
    for k in range(1, 16):
        e_in[0, 0, k].wait_recv()
    combine(0, 0)
    for p in (1, 2):
        for k in range(1, 16):
            e_in[p, 0, k].wait_recv()
        combine(p, 0)
    for p in range(3):
        give(p, 0)
    for copy in p_in:
        copy.wait_recv()
    for p in range(3):
        columns = slice(OFF[p], OFF[p] + COLS[p])
        total = pj_s[:, columns] + pf[p][0]
        for d in range(1, 4):
            total = total + pr[p][d].astype(F32)
        out_ref[:, columns] = total
    for copy in sent:
        copy.wait_send()


def layer(queries, key_rows, values, out_weight, expert_ids, gate_ints, w_gate, w_up, w_down):
    count = queries.shape[0] // CHUNK
    blocks = [a.reshape(count, CHUNK, 128) for a in (queries, key_rows, values)]
    vm = pltpu.VMEM
    sem = lambda n: pltpu.SemaphoreType.DMA((n,))
    by = lambda *lead: [vm((*lead, n), BF) for n in COLS]
    scratch = [
        vm((count, CHUNK, 128), F32), vm((count, CHUNK, 128), F32), vm((count, CHUNK, 128), F32),
        vm((count, CHUNK, 128), F32), vm((128, 128), BF), vm((4, 128, 128), BF),
        vm((4, 2, 4, 64, 128), BF), vm((4, 2, 4, 64, 128), BF), vm((4, 2, 4, 64, 128), BF),
        vm((4, 2, 128, HALF), BF), vm((4, 2, 128, HALF), BF),
        vm((CB, 4, 64, CBW), BF), vm((CB, 4, 64, CBW), BF), vm((CB, 4, 64, CBW), F32), vm((64, 2048), F32),
        vm((16, 128), BF), vm((4, 2, 16, 128), BF), vm((4, 2, 16, 128), BF), vm((4, 2, 16, 128), BF),
        vm((3, 4, 256, 128), BF), vm((3, 4, 128, 256), BF),
        *by(4, 2, 64), *by(4, 16, 16), *by(4, 4, 4, 16), *by(4, 4, 4, 16), *by(4, 16, 16),
        *[vm((4, 64, n), F32) for n in COLS], *by(4, 64), *by(4, 64), *by(4, 64), *by(4, 64),
        vm((2048, 768), BF), vm((2048, 768), BF), vm((768, 2048), BF),
        sem(8), sem(4), sem(4), sem(16), sem(16), sem(8), sem(8), sem(16), sem(16), sem(16), sem(16),
        sem(24), sem(24), sem(24), sem(24), sem(192), sem(192), sem(192), sem(192),
        sem(12), sem(12), sem(12), sem(12), sem(8), sem(8), sem(32), sem(32),
    ]
    hbm = pl.BlockSpec(memory_space=pl.ANY)
    vmem = pl.BlockSpec(memory_space=pltpu.VMEM)
    return pl.pallas_call(
        body,
        out_shape=jax.ShapeDtypeStruct((64, 2048), F32),
        in_specs=[hbm, hbm, hbm, hbm, vmem, vmem, hbm, hbm, hbm],
        out_specs=vmem,
        scratch_shapes=scratch,
        compiler_params=pltpu.CompilerParams(
            collective_id=0, has_side_effects=True, vmem_limit_bytes=62 << 20
        ),
        cost_estimate=pl.CostEstimate(flops=13 * 10**9, bytes_accessed=14 * 10**6, transcendentals=10**6),
    )(*blocks, out_weight, expert_ids.T, gate_ints.T, w_gate[0], w_up[0], w_down[0])


def solution(mesh):
    placed = (
        P("seq", "head"),
        P("seq", "head"),
        P("seq", "head"),
        P("head", None),
        P(("seq", "head"), None),
        P(("seq", "head"), None),
        P(("seq", "head"), None, None),
        P(("seq", "head"), None, None),
        P(("seq", "head"), None, None),
    )
    return jax.shard_map(
        layer, mesh=mesh, in_specs=placed, out_specs=P(("seq", "head"), None), check_vma=False
    )
```

```python
import functools

import jax
import jax.numpy as jnp
from jax import lax
from jax.experimental import pallas as pl
from jax.experimental.pallas import tpu as pltpu
from jax.sharding import PartitionSpec as P

MESH = pl.DeviceIdType.MESH
BF = jnp.bfloat16
F32 = jnp.float32
COLS = (768, 640, 640)
OFF = (0, 768, 1408)
PLANE = ((1, 2), (0, 2), (0, 1))
ORDER = (5, 10, 15, 8, 2, 7, 13, 1, 4, 11, 14, 3, 12, 6, 9)
CB = 4
CBW = 512
HALF = 1024
STEPS = (1, 2, 3, 0)
CHUNK = 256


def partners():
    found = []
    for a in range(4):
        for b in range(4):
            for d in range(4):
                if 0 in (a, b, d) and (a, b, d) != (0, 0, 0):
                    found.append((a, b, d, 0))
    found.append((0, 0, 0, 1))
    for a in range(1, 4):
        found += [(a, 0, 0, 1), (0, a, 0, 1), (0, 0, a, 1)]
    return found


def body(
    q_h, k_h, v_h, w_h, ids_ref, gi_ref, wg_h, wu_h, wd_h, out_ref,
    q_s, k_s, v_s, o_s, st_s, st_r, at_s, ar0, ar1, w0, w1, rs_s, rs_r, pf_s, pj_s,
    vg_s, m0, m1, m2, sel_s, com_s, l0, l1, l2, ds0, ds1, ds2, r0, r1, r2,
    o0, o1, o2, rt0, rt1, rt2, pf0, pf1, pf2, px0, px1, px2, xr0, xr1, xr2,
    ps0, ps1, ps2, pr0, pr1, pr2, wg_s, wu_s, wd_s,
    loc_sem, st_ss, st_rs, at_ss, at_rs, w_ss, w_rs, wf_ss, wf_rs, rs_ss, rs_rs,
    m_ss, m_rs, l_ss, l_rs, d_ss, d_rs, e_ss, e_rs, x_ss, x_rs, p_ss, p_rs, q_ss, q_rs, z_ss, z_rs,
):
    meta, line = (m0, m1, m2), (l0, l1, l2)
    ds, rr, oo, rt = (ds0, ds1, ds2), (r0, r1, r2), (o0, o1, o2), (rt0, rt1, rt2)
    pf, px, xr, ps, pr = (pf0, pf1, pf2), (px0, px1, px2), (xr0, xr1, xr2), (ps0, ps1, ps2), (pr0, pr1, pr2)
    ar, ws = (ar0, ar1), (w0, w1)
    z = lax.axis_index("seq")
    head = lax.axis_index("head")
    y, x, c = head // 8, (head // 2) % 4, head % 2
    at = (x, y, z)
    other = 1 - c

    def dev(coords, core):
        return (coords[2], (coords[1] * 4 + coords[0]) * 2 + core)

    def moved(**shift):
        return tuple((at[i] + shift.get("xyz"[i], 0)) % 4 for i in range(3))

    def along(axis, d):
        return tuple((at[i] + d) % 4 if i == axis else at[i] for i in range(3))

    drains = []

    def remote(src, dst, ss, rs, device):
        return pltpu.make_async_remote_copy(
            src_ref=src, dst_ref=dst, send_sem=ss, recv_sem=rs, device_id=device, device_id_type=MESH
        )

    def send(*what):
        copy = remote(*what)
        copy.start()
        return copy

    def arrived(ref, sem):
        pltpu.make_async_copy(ref, ref, sem).wait()

    def keep(src, dst, sem):
        pltpu.make_async_copy(src, dst, sem).start()

    loads = []
    for i, (src, dst) in enumerate(
        (
            (k_h, k_s), (v_h, v_s), (w_h.at[:, :HALF], w0.at[y, c]), (w_h.at[:, HALF:], w1.at[x, c]),
            (q_h, q_s), (wg_h, wg_s), (wu_h, wu_s), (wd_h, wd_s),
        )
    ):
        copy = pltpu.make_async_copy(src, dst, loc_sem.at[i])
        copy.start()
        loads.append(copy)

    barrier = pltpu.get_barrier_semaphore()
    greeted = partners()
    for dx, dy, dz, dc in greeted:
        core = other if dc else c
        pl.semaphore_signal(
            barrier, inc=1, device_id=dev(moved(x=dx, y=dy, z=dz), core), device_id_type=MESH
        )

    ids = ids_ref[...]
    experts = lax.broadcasted_iota(jnp.int32, (128, 64), 0)
    gates = gi_ref[...].astype(F32)
    gates = gates / jnp.sum(gates, axis=0, keepdims=True)
    named = jnp.zeros((128, 64), F32)
    for k in range(8):
        named = jnp.where(ids[k : k + 1] == experts, 1.0, named)
    before = (
        lax.broadcasted_iota(jnp.int32, (64, 64), 0) < lax.broadcasted_iota(jnp.int32, (64, 64), 1)
    ).astype(F32).astype(BF)
    rank = jnp.dot(named.astype(BF), before, preferred_element_type=F32)
    ranks = jnp.concatenate(
        [
            jnp.sum(jnp.where(ids[k : k + 1] == experts, rank, 0.0), axis=0, keepdims=True)
            for k in range(8)
        ],
        axis=0,
    )
    upper = jnp.concatenate([ids.astype(F32), gates], axis=1)
    under = jnp.concatenate([ranks, ranks], axis=1)
    vg_s[...] = jnp.concatenate([upper, under], axis=0).astype(BF)

    loads[0].wait()
    loads[1].wait()
    count = q_s.shape[0]
    state = jnp.zeros((128, 128), F32)
    prefix = []
    for i in range(count):
        prefix.append(state)
        state = state + lax.dot_general(
            k_s[i].astype(BF), v_s[i].astype(BF), (((0,), (0,)), ((), ())), preferred_element_type=F32
        )
    st_s[...] = state.astype(BF)
    loads[2].wait()
    loads[3].wait()

    pl.semaphore_wait(barrier, len(greeted))

    for d in (1, 2, 3):
        send(st_s, st_r.at[z], st_ss.at[0], st_rs.at[0], dev(along(2, d), c))
    drains.append((st_r.at[1:4], st_ss.at[0]))
    lines = (1, 0)

    def straight(v, a):
        return ws[v].at[a, c, :, :CBW]

    def quarter(v, a):
        return ws[v].at[a, c, :, pl.ds(pl.multiple_of(CBW + 128 * z, 128), 128)]

    w_in, q_in = {}, {}
    for d in (2, 1, 3):
        for v in range(2):
            i = v * 4 + d
            mine = quarter(v, at[lines[v]])
            q_in[v, d] = send(mine, mine, q_ss.at[v], q_rs.at[i], dev(along(lines[v], d), c))
    for d in (2, 1, 3):
        for v in range(2):
            i = v * 4 + d
            mine = straight(v, at[lines[v]])
            w_in[v, d] = send(mine, mine, w_ss.at[v], w_rs.at[i], dev(along(lines[v], d), c))

    def hand_on(v, d, half):
        got = ws[v].at[(at[lines[v]] - d + 4) % 4, c, :, half * CBW : (half + 1) * CBW]
        i = half * 2 + v
        send(got, got, wf_ss.at[i], wf_rs.at[i], dev(at, other))

    for v in range(2):
        for half in range(2):
            hand_on(v, 0, half)
            drains.append((ws[v].at[:, 0, :, :CBW], wf_ss.at[half * 2 + v]))
        drains.append((ws[v].at[1:4, 0, :, :CBW], w_ss.at[v]))
        drains.append((ws[v].at[1:4, 0, :, :128], q_ss.at[v]))
        drains.append((ws[v].at[1:4, 0, :, :384], z_ss.at[v]))
    for p in range(3):
        keep(vg_s, meta[p].at[0, c], m_rs.at[p])
        for i in range(1, 8):
            d, k = i // 2, i % 2
            send(
                vg_s, meta[p].at[(4 - d) % 4, c], m_ss.at[p * 2 + k], m_rs.at[p],
                dev(along(p, d), other if k else c),
            )
        drains.append((meta[p].at[1:4, 0], m_ss.at[p * 2]))
        drains.append((meta[p].at[:, 0], m_ss.at[p * 2 + 1]))

    loads[4].wait()
    lower = lax.broadcasted_iota(jnp.int32, (CHUNK, CHUNK), 1) <= lax.broadcasted_iota(
        jnp.int32, (CHUNK, CHUNK), 0
    )
    for i in range(count):
        qb, kb = q_s[i].astype(BF), k_s[i].astype(BF)
        scores = lax.dot_general(qb, kb, (((1,), (1,)), ((), ())), preferred_element_type=F32)
        scores = jnp.where(lower, scores, 0.0).astype(BF)
        o_s[i] = jnp.dot(scores, v_s[i].astype(BF), preferred_element_type=F32)
    for d in (1, 3, 2):
        for v in range(2):
            q_in[v, d].wait_recv()
            got = quarter(v, (at[lines[v]] - d + 4) % 4)
            for e in (2, 1, 3):
                send(got, got, z_ss.at[v], z_rs.at[v * 4 + d], dev(along(2, e), c))
    arrived(st_r.at[1:4], st_rs.at[0])
    earlier = jnp.zeros((128, 128), F32)
    for d in (1, 2, 3):
        source = (z - d + 4) % 4
        earlier = earlier + jnp.where(source < z, st_r[source].astype(F32), 0.0)
    for i in range(count):
        total = (prefix[i] + earlier).astype(BF)
        mixed = o_s[i] + jnp.dot(q_s[i].astype(BF), total, preferred_element_type=F32)
        mixed = mixed * lax.rsqrt(jnp.mean(mixed * mixed, axis=-1, keepdims=True) + 1e-06)
        mixed = mixed.astype(BF)
        for j in range(2):
            for k in range(2):
                at_s[i // 2, k, (i % 2) * 2 + j] = mixed[(2 * j + k) * 64 : (2 * j + k + 1) * 64]
    for v in range(2):
        own = at_s.at[y, c] if v == 0 else at_s.at[:, c, x]
        keep(own, ar[v].at[at[lines[v]], c], at_rs.at[v])
    for i in (4, 5, 2, 3, 6, 7, 1):
        d, k = i // 2, i % 2
        core = other if k else c
        for v in range(2):
            to = (at[lines[v]] + d) % 4
            src = at_s.at[to, core] if v == 0 else at_s.at[:, core, to]
            send(
                src, ar[v].at[at[lines[v]], c], at_ss.at[v if d else 2], at_rs.at[v],
                dev(along(lines[v], d), core),
            )
    drains.append((ar0.at[1:4], at_ss.at[0]))
    drains.append((ar1.at[1:4], at_ss.at[1]))
    drains.append((ar0.at[0], at_ss.at[2]))

    for p in range(3):
        arrived(meta[p], m_rs.at[p])
    row_r = lax.broadcasted_iota(jnp.int32, (256, 128), 0)
    base = lax.broadcasted_iota(jnp.int32, (8, 128), 1) // 64 * 1024
    first, second = row_r // 64, (row_r // 16) % 4
    for p in range(3):
        one, two = (first + at[PLANE[p][0]]) % 4, (second + at[PLANE[p][1]]) % 4
        if p == 0:
            expert = two * 32 + one * 8 + x * 2 + c
        elif p == 1:
            expert = two * 32 + y * 8 + one * 2 + c
        else:
            expert = z * 32 + two * 8 + one * 2 + c
        wanted = (row_r // 8) % 2 * 1024 + expert * 8 + row_r % 8

        def make(d, carry, p=p, wanted=wanted):
            both = meta[p][d].astype(F32)
            code = jnp.concatenate([both[0, :8, :64], both[1, :8, :64]], axis=1) * 8.0
            code = code + jnp.concatenate([both[0, 8:, :64], both[1, 8:, :64]], axis=1)
            code = code.astype(jnp.int32) + base
            weight = jnp.concatenate([both[0, :8, 64:], both[1, :8, 64:]], axis=1)
            sel = jnp.zeros((256, 128), F32)
            com = jnp.zeros((256, 128), F32)
            for k in range(8):
                hit = code[k : k + 1] == wanted
                sel = jnp.where(hit, 1.0, sel)
                com = jnp.where(hit, weight[k : k + 1], com)
            sel_s[p, d] = sel.astype(BF)
            com_s[p, d] = com.T.astype(BF)
            return carry

        lax.fori_loop(0, 4, make, 0)

    for d in (1, 3, 2):
        for v in range(2):
            w_in[v, d].wait_recv()
            hand_on(v, d, 0)
    for d in (1, 3, 2):
        for v in range(2):
            arrived(ws[v].at[0, 0, :, :384], z_rs.at[v * 4 + d])
            hand_on(v, d, 1)
    for v in range(2):
        arrived(ar[v], at_rs.at[v])
    lhs = [
        jnp.concatenate([ar[v][i // 2, i % 2].reshape(256, 128) for i in range(8)], axis=1)
        for v in range(2)
    ]
    for b in range(CB):
        v, low = b % 2, (b // 2) * CBW
        arrived(ws[v].at[:, 0, :, :CBW], wf_rs.at[b])
        part = jnp.dot(
            lhs[v], ws[v][:, :, :, low : low + CBW].reshape(1024, CBW), preferred_element_type=F32
        ).reshape(4, 64, CBW)
        pf_s[b] = part
        rs_s[b] = part.astype(BF)
        for d in (2, 1, 3):
            send(
                rs_s.at[b, (at[v] + d) % 4], rs_r.at[b, at[v]], rs_ss.at[0], rs_rs.at[b],
                dev(along(v, d), c),
            )
    drains.append((rs_r.at[:, 1:4], rs_ss.at[0]))
    square = jnp.zeros((64, 1), F32)
    for b in range(CB):
        v, low = b % 2, (b % 2) * HALF + (b // 2) * CBW
        arrived(rs_r.at[b, 1:4], rs_rs.at[b])
        total = pf_s[b, at[v]]
        for d in (1, 2, 3):
            total = total + rs_r[b, (at[v] - d + 4) % 4].astype(F32)
        pj_s[:, low : low + CBW] = total
        square = square + jnp.sum(total * total, axis=-1, keepdims=True)
    scale = lax.rsqrt(square / 2048.0 + 1e-06)

    line_in = {}
    for p in range(3):
        line[p][0, c] = (pj_s[:, OFF[p] : OFF[p] + COLS[p]] * scale).astype(BF)

    def pass_on(p, d):
        block = line[p].at[(4 - d) % 4, c]
        i = p * 8 + d * 2 + 1
        line_in[p, d * 2 + 1] = send(block, block, l_ss.at[p * 2 + 1], l_rs.at[i], dev(at, other))

    for p in (1, 2, 0):
        pass_on(p, 0)
    for d in (2, 1, 3):
        for p in (1, 2, 0):
            own = line[p].at[0, c]
            i = p * 8 + d * 2
            line_in[p, d * 2] = send(
                own, line[p].at[4 - d, c], l_ss.at[p * 2], l_rs.at[i], dev(along(p, d), c)
            )
    for p in range(3):
        drains.append((line[p].at[1:4, 0], l_ss.at[p * 2]))
        drains.append((line[p].at[:, 0], l_ss.at[p * 2 + 1]))

    def pick(p, rel):
        line_in[p, (4 - rel) % 4 * 2 + 1].wait_recv()
        picked = jnp.dot(
            sel_s[p, rel], line[p][rel].reshape(128, COLS[p]), preferred_element_type=F32
        )
        ds[p][rel] = picked.astype(BF).reshape(16, 16, COLS[p])

    def minus(k):
        return (4 - k // 4) % 4 * 4 + (4 - k % 4) % 4

    def plane_dev(p, k):
        coords = [None] * 3
        coords[p] = at[p]
        coords[PLANE[p][0]] = (at[PLANE[p][0]] + k // 4) % 4
        coords[PLANE[p][1]] = (at[PLANE[p][1]] + k % 4) % 4
        return dev(coords, c)

    def rows(ref, p, part, first, second):
        if p == 0:
            return ref.at[part, first, second]
        which = 0 if part == 0 else slice(1, 4)
        return ref.at[first, which, second] if p == 1 else ref.at[first, second, which]

    def blocks(ref, p, part, k):
        if p == 0 or part == 0:
            return ref.at[part, k]
        return ref.at[1:4, k]

    def group(p, part):
        return part if p == 0 else 2 + p * 2 + part

    def step_of(p, part, k):
        return part if p == 0 else (4 - k // 4) % 4

    def out(p, part, k):
        n = minus(k)
        return (
            blocks(ds[p], p, part, k), rows(rr[p], p, part, n // 4, n % 4), d_ss.at[group(p, part)],
            d_rs.at[p * 4 + step_of(p, part, k)], plane_dev(p, k),
        )

    def back(p, part, k):
        return (
            rows(oo[p], p, part, k // 4, k % 4), blocks(rt[p], p, part, minus(k)), e_ss.at[group(p, part)],
            e_rs.at[group(p, part)], plane_dev(p, k),
        )

    def go(p, part, k):
        if k:
            send(*out(p, part, k))
        else:
            src, dst, _, sem, _ = out(p, part, k)
            keep(src, dst, sem)

    def come(p, part, k):
        if k:
            send(*back(p, part, k))
        else:
            src, dst, _, sem, _ = back(p, part, k)
            keep(src, dst, sem)

    for p in range(3):
        for part in range(4 if p == 0 else 2):
            whole = ds[p].at[part, 1:16] if p == 0 or part == 0 else ds[p].at[1:4, 1:16]
            drains.append((whole, d_ss.at[group(p, part)]))
            drains.append((whole, e_ss.at[group(p, part)]))

    for p in (1, 2, 0):
        pick(p, 0)
        for k in (*ORDER, 0):
            go(p, 0, k)
    for d in (1, 3, 2):
        for p in (1, 2, 0):
            line_in[p, d * 2].wait_recv()
            pass_on(p, d)
    for rel in (3, 1, 2):
        for p in (1, 2):
            pick(p, rel)
    for i in STEPS:
        if i:
            pick(0, i)
            go(0, i, 0)
        for b in (2, 1, 3, 0):
            k = (4 - i) % 4 * 4 + b
            go(1, 1, k)
            go(2, 1, k)
            if i:
                for k in ORDER[b * 4 : b * 4 + 4]:
                    go(0, i, k)
    for copy in loads[5:]:
        copy.wait()

    def expert_rows(i):
        taken = [rr[p][i].reshape(256, COLS[p]) for p in range(3)]
        gate_val = jnp.zeros((256, 768), F32)
        up_val = jnp.zeros((256, 768), F32)
        for p in range(3):
            gate_val = gate_val + jnp.dot(
                taken[p], wg_s[OFF[p] : OFF[p] + COLS[p]], preferred_element_type=F32
            )
            up_val = up_val + jnp.dot(
                taken[p], wu_s[OFF[p] : OFF[p] + COLS[p]], preferred_element_type=F32
            )
        act = (gate_val / (1.0 + jnp.exp(-gate_val)) * up_val).astype(BF)
        for p in range(3):
            result = jnp.dot(act, wd_s[:, OFF[p] : OFF[p] + COLS[p]], preferred_element_type=F32)
            oo[p][i] = result.astype(BF).reshape(4, 4, 16, COLS[p])

    for i in STEPS:
        for p in range(3):
            arrived(rr[p].at[i], d_rs.at[p * 4 + i])
        expert_rows(i)
        come(0, i, 0)
        for b in (2, 1, 3, 0):
            k = i * 4 + b
            come(1, 1, k)
            come(2, 1, k)
            for k in ORDER[b * 4 : b * 4 + 4]:
                come(0, i, k)
    for k in (*ORDER, 0):
        for p in (1, 2):
            come(p, 0, k)

    x_in = {}

    def combine(p, d):
        sums = jnp.dot(
            com_s[p, d], rt[p][d].reshape(256, COLS[p]), preferred_element_type=F32
        ).reshape(2, 64, COLS[p])
        pf[p][d] = jnp.where(c == 0, sums[0], sums[1])
        px[p][d] = jnp.where(c == 0, sums[1], sums[0]).astype(BF)
        i = p * 4 + d
        x_in[p, d] = send(px[p].at[d], xr[p].at[d], x_ss.at[p], x_rs.at[i], dev(at, other))

    def give(p, d):
        x_in[p, d].wait_recv()
        total = pf[p][d] + xr[p][d].astype(F32)
        if d == 0:
            pf[p][d] = total
            return
        ps[p][d] = total.astype(BF)
        send(ps[p].at[d], pr[p].at[d], p_ss.at[p], p_rs.at[p], dev(along(p, d), c))

    for i in STEPS[:3]:
        arrived(rt0.at[i], e_rs.at[group(0, i)])
        combine(0, i)
    for d in STEPS[:3]:
        give(0, d)
    for p in (1, 2):
        arrived(rt[p].at[1:4], e_rs.at[group(p, 1)])
    for d in (2, 1, 3):
        for p in (1, 2):
            combine(p, d)
    for d in (2, 1, 3):
        for p in (1, 2):
            give(p, d)
    for p in range(3):
        arrived(rt[p].at[0], e_rs.at[group(p, 0)])
        combine(p, 0)
        drains.append((xr[p], x_ss.at[p]))
        drains.append((pr[p].at[1:4], p_ss.at[p]))
    for p in range(3):
        give(p, 0)
        arrived(pr[p].at[1:4], p_rs.at[p])
    for p in range(3):
        columns = slice(OFF[p], OFF[p] + COLS[p])
        total = pj_s[:, columns] + pf[p][0]
        for d in range(1, 4):
            total = total + pr[p][d].astype(F32)
        out_ref[:, columns] = total
    for ref, sem in drains:
        arrived(ref, sem)


def layer(queries, key_rows, values, out_weight, expert_ids, gate_ints, w_gate, w_up, w_down):
    count = queries.shape[0] // CHUNK
    blocks = [a.reshape(count, CHUNK, 128) for a in (queries, key_rows, values)]
    vm = pltpu.VMEM
    sem = lambda n: pltpu.SemaphoreType.DMA((n,))
    by = lambda *lead: [vm((*lead, n), BF) for n in COLS]
    scratch = [
        vm((count, CHUNK, 128), F32), vm((count, CHUNK, 128), F32), vm((count, CHUNK, 128), F32),
        vm((count, CHUNK, 128), F32), vm((128, 128), BF), vm((4, 128, 128), BF),
        vm((4, 2, 4, 64, 128), BF), vm((4, 2, 4, 64, 128), BF), vm((4, 2, 4, 64, 128), BF),
        vm((4, 2, 128, HALF), BF), vm((4, 2, 128, HALF), BF),
        vm((CB, 4, 64, CBW), BF), vm((CB, 4, 64, CBW), BF), vm((CB, 4, 64, CBW), F32), vm((64, 2048), F32),
        vm((16, 128), BF), vm((4, 2, 16, 128), BF), vm((4, 2, 16, 128), BF), vm((4, 2, 16, 128), BF),
        vm((3, 4, 256, 128), BF), vm((3, 4, 128, 256), BF),
        *by(4, 2, 64), *by(4, 16, 16), *by(4, 4, 4, 16), *by(4, 4, 4, 16), *by(4, 16, 16),
        *[vm((4, 64, n), F32) for n in COLS], *by(4, 64), *by(4, 64), *by(4, 64), *by(4, 64),
        vm((2048, 768), BF), vm((2048, 768), BF), vm((768, 2048), BF),
        sem(8), sem(1), sem(1), sem(3), sem(2), sem(2), sem(8), sem(4), sem(4), sem(1), sem(4),
        sem(6), sem(3), sem(6), sem(24), sem(8), sem(12), sem(8), sem(8),
        sem(3), sem(12), sem(3), sem(3), sem(2), sem(8), sem(2), sem(8),
    ]
    hbm = pl.BlockSpec(memory_space=pl.ANY)
    vmem = pl.BlockSpec(memory_space=pltpu.VMEM)
    return pl.pallas_call(
        body,
        out_shape=jax.ShapeDtypeStruct((64, 2048), F32),
        in_specs=[hbm, hbm, hbm, hbm, vmem, vmem, hbm, hbm, hbm],
        out_specs=vmem,
        scratch_shapes=scratch,
        compiler_params=pltpu.CompilerParams(
            collective_id=0, has_side_effects=True, vmem_limit_bytes=62 << 20
        ),
        cost_estimate=pl.CostEstimate(flops=13 * 10**9, bytes_accessed=14 * 10**6, transcendentals=10**6),
    )(*blocks, out_weight, expert_ids.T, gate_ints.T, w_gate[0], w_up[0], w_down[0])


def solution(mesh):
    placed = (
        P("seq", "head"),
        P("seq", "head"),
        P("seq", "head"),
        P("head", None),
        P(("seq", "head"), None),
        P(("seq", "head"), None),
        P(("seq", "head"), None, None),
        P(("seq", "head"), None, None),
        P(("seq", "head"), None, None),
    )
    return jax.shard_map(
        layer, mesh=mesh, in_specs=placed, out_specs=P(("seq", "head"), None), check_vma=False
    )
```

```python
import functools

import jax
import jax.numpy as jnp
from jax import lax
from jax.experimental import pallas as pl
from jax.experimental.pallas import tpu as pltpu
from jax.sharding import PartitionSpec as P

MESH = pl.DeviceIdType.MESH
BF = jnp.bfloat16
F32 = jnp.float32
COLS = (768, 640, 640)
OFF = (0, 768, 1408)
PLANE = ((1, 2), (0, 2), (0, 1))
ORDER = (5, 10, 15, 8, 2, 7, 13, 1, 4, 11, 14, 3, 12, 6, 9)
CB = 4
CBW = 512
HALF = 1024
STEPS = (2, 1, 3, 0)
CHUNK = 256


def partners():
    found = []
    for a in range(4):
        for b in range(4):
            for d in range(4):
                if 0 in (a, b, d) and (a, b, d) != (0, 0, 0):
                    found.append((a, b, d, 0))
    found.append((0, 0, 0, 1))
    for a in range(1, 4):
        found += [(a, 0, 0, 1), (0, a, 0, 1), (0, 0, a, 1)]
    return found


def body(
    q_h, k_h, v_h, w_h, ids_ref, gi_ref, wg_h, wu_h, wd_h, out_ref,
    q_s, k_s, v_s, o_s, st_s, st_r, at_s, ar0, ar1, w0, w1, rs_s, rs_r, pf_s, pj_s,
    vg_s, m0, m1, m2, sel_s, com_s, l0, l1, l2, ds0, ds1, ds2, r0, r1, r2,
    o0, o1, o2, rt0, rt1, rt2, pf0, pf1, pf2, px0, px1, px2, xr0, xr1, xr2,
    ps0, ps1, ps2, pr0, pr1, pr2, wg_s, wu_s, wd_s,
    loc_sem, st_ss, st_rs, at_ss, at_rs, w_ss, w_rs, wf_ss, wf_rs, rs_ss, rs_rs,
    m_ss, m_rs, l_ss, l_rs, d_ss, d_rs, e_ss, e_rs, x_ss, x_rs, p_ss, p_rs, q_ss, q_rs, z_ss, z_rs,
):
    meta, line = (m0, m1, m2), (l0, l1, l2)
    ds, rr, oo, rt = (ds0, ds1, ds2), (r0, r1, r2), (o0, o1, o2), (rt0, rt1, rt2)
    pf, px, xr, ps, pr = (pf0, pf1, pf2), (px0, px1, px2), (xr0, xr1, xr2), (ps0, ps1, ps2), (pr0, pr1, pr2)
    ar, ws = (ar0, ar1), (w0, w1)
    z = lax.axis_index("seq")
    head = lax.axis_index("head")
    y, x, c = head // 8, (head // 2) % 4, head % 2
    at = (x, y, z)
    other = 1 - c

    def dev(coords, core):
        return (coords[2], (coords[1] * 4 + coords[0]) * 2 + core)

    def moved(**shift):
        return tuple((at[i] + shift.get("xyz"[i], 0)) % 4 for i in range(3))

    def along(axis, d):
        return tuple((at[i] + d) % 4 if i == axis else at[i] for i in range(3))

    drains = []

    def remote(src, dst, ss, rs, device):
        return pltpu.make_async_remote_copy(
            src_ref=src, dst_ref=dst, send_sem=ss, recv_sem=rs, device_id=device, device_id_type=MESH
        )

    def send(*what):
        copy = remote(*what)
        copy.start()
        return copy

    def arrived(ref, sem):
        pltpu.make_async_copy(ref, ref, sem).wait()

    def keep(src, dst, sem):
        pltpu.make_async_copy(src, dst, sem).start()

    loads = []
    for i, (src, dst) in enumerate(
        (
            (k_h, k_s), (v_h, v_s), (w_h.at[:, :HALF], w0.at[y, c]), (w_h.at[:, HALF:], w1.at[x, c]),
            (q_h, q_s), (wg_h, wg_s), (wu_h, wu_s), (wd_h, wd_s),
        )
    ):
        copy = pltpu.make_async_copy(src, dst, loc_sem.at[i])
        copy.start()
        loads.append(copy)

    barrier = pltpu.get_barrier_semaphore()
    greeted = partners()
    for dx, dy, dz, dc in greeted:
        core = other if dc else c
        pl.semaphore_signal(
            barrier, inc=1, device_id=dev(moved(x=dx, y=dy, z=dz), core), device_id_type=MESH
        )

    ids = ids_ref[...]
    experts = lax.broadcasted_iota(jnp.int32, (128, 64), 0)
    gates = gi_ref[...].astype(F32)
    gates = gates / jnp.sum(gates, axis=0, keepdims=True)
    named = jnp.zeros((128, 64), F32)
    for k in range(8):
        named = jnp.where(ids[k : k + 1] == experts, 1.0, named)
    before = (
        lax.broadcasted_iota(jnp.int32, (64, 64), 0) < lax.broadcasted_iota(jnp.int32, (64, 64), 1)
    ).astype(F32).astype(BF)
    rank = jnp.dot(named.astype(BF), before, preferred_element_type=F32)
    ranks = jnp.concatenate(
        [
            jnp.sum(jnp.where(ids[k : k + 1] == experts, rank, 0.0), axis=0, keepdims=True)
            for k in range(8)
        ],
        axis=0,
    )
    upper = jnp.concatenate([ids.astype(F32), gates], axis=1)
    under = jnp.concatenate([ranks, ranks], axis=1)
    vg_s[...] = jnp.concatenate([upper, under], axis=0).astype(BF)

    loads[0].wait()
    loads[1].wait()
    count = q_s.shape[0]
    state = jnp.zeros((128, 128), F32)
    prefix = []
    for i in range(count):
        prefix.append(state)
        state = state + lax.dot_general(
            k_s[i].astype(BF), v_s[i].astype(BF), (((0,), (0,)), ((), ())), preferred_element_type=F32
        )
    st_s[...] = state.astype(BF)
    loads[2].wait()
    loads[3].wait()

    pl.semaphore_wait(barrier, len(greeted))

    for d in (1, 2, 3):
        send(st_s, st_r.at[z], st_ss.at[0], st_rs.at[0], dev(along(2, d), c))
    drains.append((st_r.at[1:4], st_ss.at[0]))
    lines = (1, 0)

    def straight(v, a):
        return ws[v].at[a, c, :, :CBW]

    def quarter(v, a):
        return ws[v].at[a, c, :, pl.ds(pl.multiple_of(CBW + 128 * z, 128), 128)]

    w_in, q_in = {}, {}
    for d in (2, 1, 3):
        for v in range(2):
            i = v * 4 + d
            mine = quarter(v, at[lines[v]])
            q_in[v, d] = send(mine, mine, q_ss.at[v], q_rs.at[i], dev(along(lines[v], d), c))
    for d in (2, 1, 3):
        for v in range(2):
            i = v * 4 + d
            mine = straight(v, at[lines[v]])
            w_in[v, d] = send(mine, mine, w_ss.at[v], w_rs.at[i], dev(along(lines[v], d), c))

    def hand_on(v, d, half):
        got = ws[v].at[(at[lines[v]] - d + 4) % 4, c, :, half * CBW : (half + 1) * CBW]
        i = half * 2 + v
        send(got, got, wf_ss.at[i], wf_rs.at[i], dev(at, other))

    for v in range(2):
        for half in range(2):
            hand_on(v, 0, half)
            drains.append((ws[v].at[:, 0, :, :CBW], wf_ss.at[half * 2 + v]))
        drains.append((ws[v].at[1:4, 0, :, :CBW], w_ss.at[v]))
        drains.append((ws[v].at[1:4, 0, :, :128], q_ss.at[v]))
        drains.append((ws[v].at[1:4, 0, :, :384], z_ss.at[v]))
    for p in range(3):
        keep(vg_s, meta[p].at[0, c], m_rs.at[p])
        for i in range(1, 8):
            d, k = i // 2, i % 2
            send(
                vg_s, meta[p].at[(4 - d) % 4, c], m_ss.at[p * 2 + k], m_rs.at[p],
                dev(along(p, d), other if k else c),
            )
        drains.append((meta[p].at[1:4, 0], m_ss.at[p * 2]))
        drains.append((meta[p].at[:, 0], m_ss.at[p * 2 + 1]))

    loads[4].wait()
    lower = lax.broadcasted_iota(jnp.int32, (CHUNK, CHUNK), 1) <= lax.broadcasted_iota(
        jnp.int32, (CHUNK, CHUNK), 0
    )
    for i in range(count):
        qb, kb = q_s[i].astype(BF), k_s[i].astype(BF)
        scores = lax.dot_general(qb, kb, (((1,), (1,)), ((), ())), preferred_element_type=F32)
        scores = jnp.where(lower, scores, 0.0).astype(BF)
        o_s[i] = jnp.dot(scores, v_s[i].astype(BF), preferred_element_type=F32)
        if i == 3:
            for d in (1, 3, 2):
                for v in range(2):
                    q_in[v, d].wait_recv()
                    got = quarter(v, (at[lines[v]] - d + 4) % 4)
                    for e in (2, 1, 3):
                        send(got, got, z_ss.at[v], z_rs.at[v * 4 + d], dev(along(2, e), c))
    arrived(st_r.at[1:4], st_rs.at[0])
    earlier = jnp.zeros((128, 128), F32)
    for d in (1, 2, 3):
        source = (z - d + 4) % 4
        earlier = earlier + jnp.where(source < z, st_r[source].astype(F32), 0.0)
    for i in range(count):
        total = (prefix[i] + earlier).astype(BF)
        mixed = o_s[i] + jnp.dot(q_s[i].astype(BF), total, preferred_element_type=F32)
        mixed = mixed * lax.rsqrt(jnp.mean(mixed * mixed, axis=-1, keepdims=True) + 1e-06)
        mixed = mixed.astype(BF)
        for j in range(2):
            for k in range(2):
                at_s[i // 2, k, (i % 2) * 2 + j] = mixed[(2 * j + k) * 64 : (2 * j + k + 1) * 64]
    for v in range(2):
        own = at_s.at[y, c] if v == 0 else at_s.at[:, c, x]
        keep(own, ar[v].at[at[lines[v]], c], at_rs.at[v])
    for i in (4, 5, 2, 3, 6, 7, 1):
        d, k = i // 2, i % 2
        core = other if k else c
        for v in range(2):
            to = (at[lines[v]] + d) % 4
            src = at_s.at[to, core] if v == 0 else at_s.at[:, core, to]
            send(
                src, ar[v].at[at[lines[v]], c], at_ss.at[v if d else 2], at_rs.at[v],
                dev(along(lines[v], d), core),
            )
    drains.append((ar0.at[1:4], at_ss.at[0]))
    drains.append((ar1.at[1:4], at_ss.at[1]))
    drains.append((ar0.at[0], at_ss.at[2]))

    for d in (1, 3, 2):
        for v in range(2):
            w_in[v, d].wait_recv()
            hand_on(v, d, 0)
    for d in (1, 3, 2):
        for v in range(2):
            arrived(ws[v].at[0, 0, :, :384], z_rs.at[v * 4 + d])
            hand_on(v, d, 1)
    for v in range(2):
        arrived(ar[v], at_rs.at[v])
    lhs = [
        jnp.concatenate([ar[v][i // 2, i % 2].reshape(256, 128) for i in range(8)], axis=1)
        for v in range(2)
    ]
    for b in range(CB):
        v, low = b % 2, (b // 2) * CBW
        arrived(ws[v].at[:, 0, :, :CBW], wf_rs.at[b])
        part = jnp.dot(
            lhs[v], ws[v][:, :, :, low : low + CBW].reshape(1024, CBW), preferred_element_type=F32
        ).reshape(4, 64, CBW)
        pf_s[b] = part
        rs_s[b] = part.astype(BF)
        for d in (2, 1, 3):
            send(
                rs_s.at[b, (at[v] + d) % 4], rs_r.at[b, at[v]], rs_ss.at[0], rs_rs.at[b],
                dev(along(v, d), c),
            )
    drains.append((rs_r.at[:, 1:4], rs_ss.at[0]))

    for p in range(3):
        arrived(meta[p], m_rs.at[p])
    row_r = lax.broadcasted_iota(jnp.int32, (256, 128), 0)
    base = lax.broadcasted_iota(jnp.int32, (8, 128), 1) // 64 * 1024
    first, second = row_r // 64, (row_r // 16) % 4
    for p in range(3):
        one, two = (first + at[PLANE[p][0]]) % 4, (second + at[PLANE[p][1]]) % 4
        if p == 0:
            expert = two * 32 + one * 8 + x * 2 + c
        elif p == 1:
            expert = two * 32 + y * 8 + one * 2 + c
        else:
            expert = z * 32 + two * 8 + one * 2 + c
        wanted = (row_r // 8) % 2 * 1024 + expert * 8 + row_r % 8

        def make(d, carry, p=p, wanted=wanted):
            both = meta[p][d].astype(F32)
            code = jnp.concatenate([both[0, :8, :64], both[1, :8, :64]], axis=1) * 8.0
            code = code + jnp.concatenate([both[0, 8:, :64], both[1, 8:, :64]], axis=1)
            code = code.astype(jnp.int32) + base
            weight = jnp.concatenate([both[0, :8, 64:], both[1, :8, 64:]], axis=1)
            sel = jnp.zeros((256, 128), F32)
            com = jnp.zeros((256, 128), F32)
            for k in range(8):
                hit = code[k : k + 1] == wanted
                sel = jnp.where(hit, 1.0, sel)
                com = jnp.where(hit, weight[k : k + 1], com)
            sel_s[p, d] = sel.astype(BF)
            com_s[p, d] = com.T.astype(BF)
            return carry

        lax.fori_loop(0, 4, make, 0)

    square = jnp.zeros((64, 1), F32)
    for b in range(CB):
        v, low = b % 2, (b % 2) * HALF + (b // 2) * CBW
        arrived(rs_r.at[b, 1:4], rs_rs.at[b])
        total = pf_s[b, at[v]]
        for d in (1, 2, 3):
            total = total + rs_r[b, (at[v] - d + 4) % 4].astype(F32)
        pj_s[:, low : low + CBW] = total
        square = square + jnp.sum(total * total, axis=-1, keepdims=True)
    scale = lax.rsqrt(square / 2048.0 + 1e-06)

    line_in = {}
    for p in range(3):
        line[p][0, c] = (pj_s[:, OFF[p] : OFF[p] + COLS[p]] * scale).astype(BF)

    def pass_on(p, d):
        block = line[p].at[(4 - d) % 4, c]
        i = p * 8 + d * 2 + 1
        line_in[p, d * 2 + 1] = send(block, block, l_ss.at[p * 2 + 1], l_rs.at[i], dev(at, other))

    for p in (1, 2, 0):
        pass_on(p, 0)
    for d in (2, 1, 3):
        for p in (1, 2, 0):
            own = line[p].at[0, c]
            i = p * 8 + d * 2
            line_in[p, d * 2] = send(
                own, line[p].at[4 - d, c], l_ss.at[p * 2], l_rs.at[i], dev(along(p, d), c)
            )
    for p in range(3):
        drains.append((line[p].at[1:4, 0], l_ss.at[p * 2]))
        drains.append((line[p].at[:, 0], l_ss.at[p * 2 + 1]))

    def pick(p, rel):
        line_in[p, (4 - rel) % 4 * 2 + 1].wait_recv()
        picked = jnp.dot(
            sel_s[p, rel], line[p][rel].reshape(128, COLS[p]), preferred_element_type=F32
        )
        ds[p][rel] = picked.astype(BF).reshape(16, 16, COLS[p])

    def minus(k):
        return (4 - k // 4) % 4 * 4 + (4 - k % 4) % 4

    def plane_dev(p, k):
        coords = [None] * 3
        coords[p] = at[p]
        coords[PLANE[p][0]] = (at[PLANE[p][0]] + k // 4) % 4
        coords[PLANE[p][1]] = (at[PLANE[p][1]] + k % 4) % 4
        return dev(coords, c)

    def rows(ref, p, part, first, second):
        if p == 0:
            return ref.at[part, first, second]
        which = 0 if part == 0 else slice(1, 4)
        return ref.at[first, which, second] if p == 1 else ref.at[first, second, which]

    def blocks(ref, p, part, k):
        if p == 0 or part == 0:
            return ref.at[part, k]
        return ref.at[1:4, k]

    def group(p, part):
        return part if p == 0 else 2 + p * 2 + part

    def step_of(p, part, k):
        return part if p == 0 else (4 - k // 4) % 4

    def out(p, part, k):
        n = minus(k)
        return (
            blocks(ds[p], p, part, k), rows(rr[p], p, part, n // 4, n % 4), d_ss.at[group(p, part)],
            d_rs.at[p * 4 + step_of(p, part, k)], plane_dev(p, k),
        )

    def back(p, part, k):
        return (
            rows(oo[p], p, part, k // 4, k % 4), blocks(rt[p], p, part, minus(k)), e_ss.at[group(p, part)],
            e_rs.at[group(p, part)], plane_dev(p, k),
        )

    def go(p, part, k):
        if k:
            send(*out(p, part, k))
        else:
            src, dst, _, sem, _ = out(p, part, k)
            keep(src, dst, sem)

    def come(p, part, k):
        if k:
            send(*back(p, part, k))
        else:
            src, dst, _, sem, _ = back(p, part, k)
            keep(src, dst, sem)

    for p in range(3):
        for part in range(4 if p == 0 else 2):
            whole = ds[p].at[part, 1:16] if p == 0 or part == 0 else ds[p].at[1:4, 1:16]
            drains.append((whole, d_ss.at[group(p, part)]))
            drains.append((whole, e_ss.at[group(p, part)]))

    for p in (1, 2, 0):
        pick(p, 0)
    for k in (*ORDER, 0):
        for p in (1, 2, 0):
            go(p, 0, k)
    for d in (1, 3, 2):
        for p in (1, 2, 0):
            line_in[p, d * 2].wait_recv()
            pass_on(p, d)
    for rel in (3, 1, 2):
        for p in (1, 2):
            pick(p, rel)
    for i in STEPS:
        if i:
            pick(0, i)
            go(0, i, 0)
        for b in (2, 1, 3, 0):
            k = (4 - i) % 4 * 4 + b
            go(1, 1, k)
            go(2, 1, k)
            if i:
                for k in ORDER[b * 4 : b * 4 + 4]:
                    go(0, i, k)
    for copy in loads[5:]:
        copy.wait()

    def expert_rows(i):
        taken = [rr[p][i].reshape(256, COLS[p]) for p in range(3)]
        gate_val = jnp.zeros((256, 768), F32)
        up_val = jnp.zeros((256, 768), F32)
        for p in range(3):
            gate_val = gate_val + jnp.dot(
                taken[p], wg_s[OFF[p] : OFF[p] + COLS[p]], preferred_element_type=F32
            )
            up_val = up_val + jnp.dot(
                taken[p], wu_s[OFF[p] : OFF[p] + COLS[p]], preferred_element_type=F32
            )
        act = (gate_val / (1.0 + jnp.exp(-gate_val)) * up_val).astype(BF)
        for p in range(3):
            result = jnp.dot(act, wd_s[:, OFF[p] : OFF[p] + COLS[p]], preferred_element_type=F32)
            oo[p][i] = result.astype(BF).reshape(4, 4, 16, COLS[p])

    for i in STEPS:
        for p in range(3):
            arrived(rr[p].at[i], d_rs.at[p * 4 + i])
        expert_rows(i)
        come(0, i, 0)
        for b in (2, 1, 3, 0):
            k = i * 4 + b
            come(1, 1, k)
            come(2, 1, k)
            for k in ORDER[b * 4 : b * 4 + 4]:
                come(0, i, k)
    for k in (*ORDER, 0):
        for p in (1, 2):
            come(p, 0, k)

    x_in = {}

    def combine(p, d):
        sums = jnp.dot(
            com_s[p, d], rt[p][d].reshape(256, COLS[p]), preferred_element_type=F32
        ).reshape(2, 64, COLS[p])
        pf[p][d] = jnp.where(c == 0, sums[0], sums[1])
        px[p][d] = jnp.where(c == 0, sums[1], sums[0]).astype(BF)
        i = p * 4 + d
        x_in[p, d] = send(px[p].at[d], xr[p].at[d], x_ss.at[p], x_rs.at[i], dev(at, other))

    def give(p, d):
        x_in[p, d].wait_recv()
        total = pf[p][d] + xr[p][d].astype(F32)
        if d == 0:
            pf[p][d] = total
            return
        ps[p][d] = total.astype(BF)
        send(ps[p].at[d], pr[p].at[d], p_ss.at[p], p_rs.at[p], dev(along(p, d), c))

    for i in STEPS[:3]:
        arrived(rt0.at[i], e_rs.at[group(0, i)])
        combine(0, i)
    for d in STEPS[:3]:
        give(0, d)
    for p in (1, 2):
        arrived(rt[p].at[1:4], e_rs.at[group(p, 1)])
    for d in (2, 1, 3):
        for p in (1, 2):
            combine(p, d)
    for d in (2, 1, 3):
        for p in (1, 2):
            give(p, d)
    for p in range(3):
        arrived(rt[p].at[0], e_rs.at[group(p, 0)])
        combine(p, 0)
        drains.append((xr[p], x_ss.at[p]))
        drains.append((pr[p].at[1:4], p_ss.at[p]))
    for p in range(3):
        give(p, 0)
        arrived(pr[p].at[1:4], p_rs.at[p])
    for p in range(3):
        columns = slice(OFF[p], OFF[p] + COLS[p])
        total = pj_s[:, columns] + pf[p][0]
        for d in range(1, 4):
            total = total + pr[p][d].astype(F32)
        out_ref[:, columns] = total
    for ref, sem in drains:
        arrived(ref, sem)


def layer(queries, key_rows, values, out_weight, expert_ids, gate_ints, w_gate, w_up, w_down):
    count = queries.shape[0] // CHUNK
    blocks = [a.reshape(count, CHUNK, 128) for a in (queries, key_rows, values)]
    vm = pltpu.VMEM
    sem = lambda n: pltpu.SemaphoreType.DMA((n,))
    by = lambda *lead: [vm((*lead, n), BF) for n in COLS]
    scratch = [
        vm((count, CHUNK, 128), F32), vm((count, CHUNK, 128), F32), vm((count, CHUNK, 128), F32),
        vm((count, CHUNK, 128), F32), vm((128, 128), BF), vm((4, 128, 128), BF),
        vm((4, 2, 4, 64, 128), BF), vm((4, 2, 4, 64, 128), BF), vm((4, 2, 4, 64, 128), BF),
        vm((4, 2, 128, HALF), BF), vm((4, 2, 128, HALF), BF),
        vm((CB, 4, 64, CBW), BF), vm((CB, 4, 64, CBW), BF), vm((CB, 4, 64, CBW), F32), vm((64, 2048), F32),
        vm((16, 128), BF), vm((4, 2, 16, 128), BF), vm((4, 2, 16, 128), BF), vm((4, 2, 16, 128), BF),
        vm((3, 4, 256, 128), BF), vm((3, 4, 128, 256), BF),
        *by(4, 2, 64), *by(4, 16, 16), *by(4, 4, 4, 16), *by(4, 4, 4, 16), *by(4, 16, 16),
        *[vm((4, 64, n), F32) for n in COLS], *by(4, 64), *by(4, 64), *by(4, 64), *by(4, 64),
        vm((2048, 768), BF), vm((2048, 768), BF), vm((768, 2048), BF),
        sem(8), sem(1), sem(1), sem(3), sem(2), sem(2), sem(8), sem(4), sem(4), sem(1), sem(4),
        sem(6), sem(3), sem(6), sem(24), sem(8), sem(12), sem(8), sem(8),
        sem(3), sem(12), sem(3), sem(3), sem(2), sem(8), sem(2), sem(8),
    ]
    hbm = pl.BlockSpec(memory_space=pl.ANY)
    vmem = pl.BlockSpec(memory_space=pltpu.VMEM)
    return pl.pallas_call(
        body,
        out_shape=jax.ShapeDtypeStruct((64, 2048), F32),
        in_specs=[hbm, hbm, hbm, hbm, vmem, vmem, hbm, hbm, hbm],
        out_specs=vmem,
        scratch_shapes=scratch,
        compiler_params=pltpu.CompilerParams(
            collective_id=0, has_side_effects=True, vmem_limit_bytes=62 << 20
        ),
        cost_estimate=pl.CostEstimate(flops=13 * 10**9, bytes_accessed=14 * 10**6, transcendentals=10**6),
    )(*blocks, out_weight, expert_ids.T, gate_ints.T, w_gate[0], w_up[0], w_down[0])


def solution(mesh):
    placed = (
        P("seq", "head"),
        P("seq", "head"),
        P("seq", "head"),
        P("head", None),
        P(("seq", "head"), None),
        P(("seq", "head"), None),
        P(("seq", "head"), None, None),
        P(("seq", "head"), None, None),
        P(("seq", "head"), None, None),
    )
    return jax.shard_map(
        layer, mesh=mesh, in_specs=placed, out_specs=P(("seq", "head"), None), check_vma=False
    )
```

```python
import functools

import jax
import jax.numpy as jnp
from jax import lax
from jax.experimental import pallas as pl
from jax.experimental.pallas import tpu as pltpu
from jax.sharding import PartitionSpec as P

MESH = pl.DeviceIdType.MESH
BF = jnp.bfloat16
F32 = jnp.float32
COLS = (768, 640, 640)
OFF = (0, 768, 1408)
PLANE = ((1, 2), (0, 2), (0, 1))
ORDER = (5, 10, 15, 8, 2, 7, 13, 1, 4, 11, 14, 3, 12, 6, 9)
CB = 4
CBW = 512
HALF = 1024
STEPS = (2, 1, 3, 0)
CHUNK = 256


def partners():
    found = []
    for a in range(4):
        for b in range(4):
            for d in range(4):
                if 0 in (a, b, d) and (a, b, d) != (0, 0, 0):
                    found.append((a, b, d, 0))
    found.append((0, 0, 0, 1))
    for a in range(1, 4):
        found += [(a, 0, 0, 1), (0, a, 0, 1), (0, 0, a, 1)]
    return found


def body(
    q_h, k_h, v_h, w_h, ids_ref, gi_ref, wg_h, wu_h, wd_h, out_ref,
    q_s, k_s, v_s, o_s, st_s, st_r, at_s, ar0, ar1, w0, w1, rs_s, rs_r, pf_s, pj_s,
    vg_s, m0, m1, m2, sel_s, com_s, l0, l1, l2, ds0, ds1, ds2, r0, r1, r2,
    o0, o1, o2, rt0, rt1, rt2, pf0, pf1, pf2, px0, px1, px2, xr0, xr1, xr2,
    ps0, ps1, ps2, pr0, pr1, pr2, wg_s, wu_s, wd_s,
    loc_sem, st_ss, st_rs, at_ss, at_rs, w_ss, w_rs, wf_ss, wf_rs, rs_ss, rs_rs,
    m_ss, m_rs, l_ss, l_rs, d_ss, d_rs, e_ss, e_rs, x_ss, x_rs, p_ss, p_rs, q_ss, q_rs, z_ss, z_rs,
):
    meta, line = (m0, m1, m2), (l0, l1, l2)
    ds, rr, oo, rt = (ds0, ds1, ds2), (r0, r1, r2), (o0, o1, o2), (rt0, rt1, rt2)
    pf, px, xr, ps, pr = (pf0, pf1, pf2), (px0, px1, px2), (xr0, xr1, xr2), (ps0, ps1, ps2), (pr0, pr1, pr2)
    ar, ws = (ar0, ar1), (w0, w1)
    z = lax.axis_index("seq")
    head = lax.axis_index("head")
    y, x, c = head // 8, (head // 2) % 4, head % 2
    at = (x, y, z)
    other = 1 - c

    def dev(coords, core):
        return (coords[2], (coords[1] * 4 + coords[0]) * 2 + core)

    def moved(**shift):
        return tuple((at[i] + shift.get("xyz"[i], 0)) % 4 for i in range(3))

    def along(axis, d):
        return tuple((at[i] + d) % 4 if i == axis else at[i] for i in range(3))

    drains = []

    def remote(src, dst, ss, rs, device):
        return pltpu.make_async_remote_copy(
            src_ref=src, dst_ref=dst, send_sem=ss, recv_sem=rs, device_id=device, device_id_type=MESH
        )

    def send(*what):
        copy = remote(*what)
        copy.start()
        return copy

    def arrived(ref, sem):
        pltpu.make_async_copy(ref, ref, sem).wait()

    def keep(src, dst, sem):
        pltpu.make_async_copy(src, dst, sem).start()

    loads = []
    for i, (src, dst) in enumerate(
        (
            (k_h, k_s), (v_h, v_s), (w_h.at[:, :HALF], w0.at[y, c]), (w_h.at[:, HALF:], w1.at[x, c]),
            (q_h, q_s), (wg_h, wg_s), (wu_h, wu_s), (wd_h, wd_s),
        )
    ):
        copy = pltpu.make_async_copy(src, dst, loc_sem.at[i])
        copy.start()
        loads.append(copy)

    barrier = pltpu.get_barrier_semaphore()
    greeted = partners()
    for dx, dy, dz, dc in greeted:
        core = other if dc else c
        pl.semaphore_signal(
            barrier, inc=1, device_id=dev(moved(x=dx, y=dy, z=dz), core), device_id_type=MESH
        )

    ids = ids_ref[...]
    experts = lax.broadcasted_iota(jnp.int32, (128, 64), 0)
    gates = gi_ref[...].astype(F32)
    gates = gates / jnp.sum(gates, axis=0, keepdims=True)
    named = jnp.zeros((128, 64), F32)
    for k in range(8):
        named = jnp.where(ids[k : k + 1] == experts, 1.0, named)
    before = (
        lax.broadcasted_iota(jnp.int32, (64, 64), 0) < lax.broadcasted_iota(jnp.int32, (64, 64), 1)
    ).astype(F32).astype(BF)
    rank = jnp.dot(named.astype(BF), before, preferred_element_type=F32)
    ranks = jnp.concatenate(
        [
            jnp.sum(jnp.where(ids[k : k + 1] == experts, rank, 0.0), axis=0, keepdims=True)
            for k in range(8)
        ],
        axis=0,
    )
    upper = jnp.concatenate([ids.astype(F32), gates], axis=1)
    under = jnp.concatenate([ranks, ranks], axis=1)
    vg_s[...] = jnp.concatenate([upper, under], axis=0).astype(BF)

    loads[0].wait()
    loads[1].wait()
    count = q_s.shape[0]
    state = jnp.zeros((128, 128), F32)
    prefix = []
    for i in range(count):
        prefix.append(state)
        state = state + lax.dot_general(
            k_s[i].astype(BF), v_s[i].astype(BF), (((0,), (0,)), ((), ())), preferred_element_type=F32
        )
    st_s[...] = state.astype(BF)
    loads[2].wait()
    loads[3].wait()

    pl.semaphore_wait(barrier, len(greeted))

    for d in (1, 2, 3):
        send(st_s, st_r.at[z], st_ss.at[0], st_rs.at[0], dev(along(2, d), c))
    drains.append((st_r.at[1:4], st_ss.at[0]))
    lines = (1, 0)

    def straight(v, a):
        return ws[v].at[a, c, :, :CBW]

    def quarter(v, a):
        return ws[v].at[a, c, :, pl.ds(pl.multiple_of(CBW + 128 * z, 128), 128)]

    w_in, q_in = {}, {}
    for d in (2, 1, 3):
        for v in range(2):
            i = v * 4 + d
            mine = quarter(v, at[lines[v]])
            q_in[v, d] = send(mine, mine, q_ss.at[v], q_rs.at[i], dev(along(lines[v], d), c))
    for d in (2, 1, 3):
        for v in range(2):
            i = v * 4 + d
            mine = straight(v, at[lines[v]])
            w_in[v, d] = send(mine, mine, w_ss.at[v], w_rs.at[i], dev(along(lines[v], d), c))

    def hand_on(v, d, half):
        got = ws[v].at[(at[lines[v]] - d + 4) % 4, c, :, half * CBW : (half + 1) * CBW]
        i = half * 2 + v
        send(got, got, wf_ss.at[i], wf_rs.at[i], dev(at, other))

    for v in range(2):
        for half in range(2):
            hand_on(v, 0, half)
            drains.append((ws[v].at[:, 0, :, :CBW], wf_ss.at[half * 2 + v]))
        drains.append((ws[v].at[1:4, 0, :, :CBW], w_ss.at[v]))
        drains.append((ws[v].at[1:4, 0, :, :128], q_ss.at[v]))
        drains.append((ws[v].at[1:4, 0, :, :384], z_ss.at[v]))
    for p in range(3):
        keep(vg_s, meta[p].at[0, c], m_rs.at[p])
        for i in range(1, 8):
            d, k = i // 2, i % 2
            send(
                vg_s, meta[p].at[(4 - d) % 4, c], m_ss.at[p * 2 + k], m_rs.at[p],
                dev(along(p, d), other if k else c),
            )
        drains.append((meta[p].at[1:4, 0], m_ss.at[p * 2]))
        drains.append((meta[p].at[:, 0], m_ss.at[p * 2 + 1]))

    loads[4].wait()
    lower = lax.broadcasted_iota(jnp.int32, (CHUNK, CHUNK), 1) <= lax.broadcasted_iota(
        jnp.int32, (CHUNK, CHUNK), 0
    )
    for i in range(count):
        qb, kb = q_s[i].astype(BF), k_s[i].astype(BF)
        scores = lax.dot_general(qb, kb, (((1,), (1,)), ((), ())), preferred_element_type=F32)
        scores = jnp.where(lower, scores, 0.0).astype(BF)
        o_s[i] = jnp.dot(scores, v_s[i].astype(BF), preferred_element_type=F32)
        if i == 2:
            for d in (1, 3, 2):
                for v in range(2):
                    q_in[v, d].wait_recv()
                    got = quarter(v, (at[lines[v]] - d + 4) % 4)
                    for e in (2, 1, 3):
                        send(got, got, z_ss.at[v], z_rs.at[v * 4 + d], dev(along(2, e), c))
    arrived(st_r.at[1:4], st_rs.at[0])
    earlier = jnp.zeros((128, 128), F32)
    for d in (1, 2, 3):
        source = (z - d + 4) % 4
        earlier = earlier + jnp.where(source < z, st_r[source].astype(F32), 0.0)
    for i in range(count):
        total = (prefix[i] + earlier).astype(BF)
        mixed = o_s[i] + jnp.dot(q_s[i].astype(BF), total, preferred_element_type=F32)
        mixed = mixed * lax.rsqrt(jnp.mean(mixed * mixed, axis=-1, keepdims=True) + 1e-06)
        mixed = mixed.astype(BF)
        for j in range(2):
            for k in range(2):
                at_s[i // 2, k, (i % 2) * 2 + j] = mixed[(2 * j + k) * 64 : (2 * j + k + 1) * 64]
    for v in range(2):
        own = at_s.at[y, c] if v == 0 else at_s.at[:, c, x]
        keep(own, ar[v].at[at[lines[v]], c], at_rs.at[v])
    for i in (4, 5, 2, 3, 6, 7, 1):
        d, k = i // 2, i % 2
        core = other if k else c
        for v in range(2):
            to = (at[lines[v]] + d) % 4
            src = at_s.at[to, core] if v == 0 else at_s.at[:, core, to]
            send(
                src, ar[v].at[at[lines[v]], c], at_ss.at[v if d else 2], at_rs.at[v],
                dev(along(lines[v], d), core),
            )
    drains.append((ar0.at[1:4], at_ss.at[0]))
    drains.append((ar1.at[1:4], at_ss.at[1]))
    drains.append((ar0.at[0], at_ss.at[2]))

    for d in (1, 3, 2):
        for v in range(2):
            w_in[v, d].wait_recv()
            hand_on(v, d, 0)
    for d in (1, 3, 2):
        for v in range(2):
            arrived(ws[v].at[0, 0, :, :384], z_rs.at[v * 4 + d])
            hand_on(v, d, 1)
    for v in range(2):
        arrived(ar[v], at_rs.at[v])
    lhs = [
        jnp.concatenate([ar[v][i // 2, i % 2].reshape(256, 128) for i in range(8)], axis=1)
        for v in range(2)
    ]
    for b in range(CB):
        v, low = b % 2, (b // 2) * CBW
        arrived(ws[v].at[:, 0, :, :CBW], wf_rs.at[b])
        part = jnp.dot(
            lhs[v], ws[v][:, :, :, low : low + CBW].reshape(1024, CBW), preferred_element_type=F32
        ).reshape(4, 64, CBW)
        pf_s[b] = part
        rs_s[b] = part.astype(BF)
        for d in (2, 1, 3):
            send(
                rs_s.at[b, (at[v] + d) % 4], rs_r.at[b, at[v]], rs_ss.at[0], rs_rs.at[b],
                dev(along(v, d), c),
            )
    drains.append((rs_r.at[:, 1:4], rs_ss.at[0]))

    for p in range(3):
        arrived(meta[p], m_rs.at[p])
    row_r = lax.broadcasted_iota(jnp.int32, (256, 128), 0)
    base = lax.broadcasted_iota(jnp.int32, (8, 128), 1) // 64 * 1024
    first, second = row_r // 64, (row_r // 16) % 4
    for p in range(3):
        one, two = (first + at[PLANE[p][0]]) % 4, (second + at[PLANE[p][1]]) % 4
        if p == 0:
            expert = two * 32 + one * 8 + x * 2 + c
        elif p == 1:
            expert = two * 32 + y * 8 + one * 2 + c
        else:
            expert = z * 32 + two * 8 + one * 2 + c
        wanted = (row_r // 8) % 2 * 1024 + expert * 8 + row_r % 8

        def make(d, carry, p=p, wanted=wanted):
            both = meta[p][d].astype(F32)
            code = jnp.concatenate([both[0, :8, :64], both[1, :8, :64]], axis=1) * 8.0
            code = code + jnp.concatenate([both[0, 8:, :64], both[1, 8:, :64]], axis=1)
            code = code.astype(jnp.int32) + base
            weight = jnp.concatenate([both[0, :8, 64:], both[1, :8, 64:]], axis=1)
            sel = jnp.zeros((256, 128), F32)
            com = jnp.zeros((256, 128), F32)
            for k in range(8):
                hit = code[k : k + 1] == wanted
                sel = jnp.where(hit, 1.0, sel)
                com = jnp.where(hit, weight[k : k + 1], com)
            sel_s[p, d] = sel.astype(BF)
            com_s[p, d] = com.T.astype(BF)
            return carry

        lax.fori_loop(0, 4, make, 0)

    square = jnp.zeros((64, 1), F32)
    for b in range(CB):
        v, low = b % 2, (b % 2) * HALF + (b // 2) * CBW
        arrived(rs_r.at[b, 1:4], rs_rs.at[b])
        total = pf_s[b, at[v]]
        for d in (1, 2, 3):
            total = total + rs_r[b, (at[v] - d + 4) % 4].astype(F32)
        pj_s[:, low : low + CBW] = total
        square = square + jnp.sum(total * total, axis=-1, keepdims=True)
    scale = lax.rsqrt(square / 2048.0 + 1e-06)

    line_in = {}
    for p in range(3):
        line[p][0, c] = (pj_s[:, OFF[p] : OFF[p] + COLS[p]] * scale).astype(BF)

    def pass_on(p, d):
        block = line[p].at[(4 - d) % 4, c]
        i = p * 8 + d * 2 + 1
        line_in[p, d * 2 + 1] = send(block, block, l_ss.at[p * 2 + 1], l_rs.at[i], dev(at, other))

    for d in (2, 1, 3):
        for p in (1, 2, 0):
            own = line[p].at[0, c]
            i = p * 8 + d * 2
            line_in[p, d * 2] = send(
                own, line[p].at[4 - d, c], l_ss.at[p * 2], l_rs.at[i], dev(along(p, d), c)
            )
    for p in (1, 2, 0):
        pass_on(p, 0)
    for p in range(3):
        drains.append((line[p].at[1:4, 0], l_ss.at[p * 2]))
        drains.append((line[p].at[:, 0], l_ss.at[p * 2 + 1]))

    def pick(p, rel):
        line_in[p, (4 - rel) % 4 * 2 + 1].wait_recv()
        picked = jnp.dot(
            sel_s[p, rel], line[p][rel].reshape(128, COLS[p]), preferred_element_type=F32
        )
        ds[p][rel] = picked.astype(BF).reshape(16, 16, COLS[p])

    def minus(k):
        return (4 - k // 4) % 4 * 4 + (4 - k % 4) % 4

    def plane_dev(p, k):
        coords = [None] * 3
        coords[p] = at[p]
        coords[PLANE[p][0]] = (at[PLANE[p][0]] + k // 4) % 4
        coords[PLANE[p][1]] = (at[PLANE[p][1]] + k % 4) % 4
        return dev(coords, c)

    def rows(ref, p, part, first, second):
        if p == 0:
            return ref.at[part, first, second]
        which = 0 if part == 0 else slice(1, 4)
        return ref.at[first, which, second] if p == 1 else ref.at[first, second, which]

    def blocks(ref, p, part, k):
        if p == 0 or part == 0:
            return ref.at[part, k]
        return ref.at[1:4, k]

    def group(p, part):
        return part if p == 0 else 2 + p * 2 + part

    def step_of(p, part, k):
        return part if p == 0 else (4 - k // 4) % 4

    def out(p, part, k):
        n = minus(k)
        return (
            blocks(ds[p], p, part, k), rows(rr[p], p, part, n // 4, n % 4), d_ss.at[group(p, part)],
            d_rs.at[p * 4 + step_of(p, part, k)], plane_dev(p, k),
        )

    def back(p, part, k):
        return (
            rows(oo[p], p, part, k // 4, k % 4), blocks(rt[p], p, part, minus(k)), e_ss.at[group(p, part)],
            e_rs.at[group(p, part)], plane_dev(p, k),
        )

    def go(p, part, k):
        if k:
            send(*out(p, part, k))
        else:
            src, dst, _, sem, _ = out(p, part, k)
            keep(src, dst, sem)

    def come(p, part, k):
        if k:
            send(*back(p, part, k))
        else:
            src, dst, _, sem, _ = back(p, part, k)
            keep(src, dst, sem)

    for p in range(3):
        for part in range(4 if p == 0 else 2):
            whole = ds[p].at[part, 1:16] if p == 0 or part == 0 else ds[p].at[1:4, 1:16]
            drains.append((whole, d_ss.at[group(p, part)]))
            drains.append((whole, e_ss.at[group(p, part)]))

    for p in (1, 2, 0):
        pick(p, 0)
    for k in (*ORDER, 0):
        for p in (1, 2, 0):
            go(p, 0, k)
    for d in (1, 3, 2):
        for p in (1, 2, 0):
            line_in[p, d * 2].wait_recv()
            pass_on(p, d)
    for rel in (3, 1, 2):
        for p in (1, 2):
            pick(p, rel)
    for i in STEPS:
        if i:
            pick(0, i)
            go(0, i, 0)
        for b in (2, 1, 3, 0):
            k = (4 - i) % 4 * 4 + b
            go(1, 1, k)
            go(2, 1, k)
            if i:
                for k in ORDER[b * 4 : b * 4 + 4]:
                    go(0, i, k)
    for copy in loads[5:]:
        copy.wait()

    def expert_rows(i):
        taken = [rr[p][i].reshape(256, COLS[p]) for p in range(3)]
        gate_val = jnp.zeros((256, 768), F32)
        up_val = jnp.zeros((256, 768), F32)
        for p in range(3):
            gate_val = gate_val + jnp.dot(
                taken[p], wg_s[OFF[p] : OFF[p] + COLS[p]], preferred_element_type=F32
            )
            up_val = up_val + jnp.dot(
                taken[p], wu_s[OFF[p] : OFF[p] + COLS[p]], preferred_element_type=F32
            )
        act = (gate_val / (1.0 + jnp.exp(-gate_val)) * up_val).astype(BF)
        for p in range(3):
            result = jnp.dot(act, wd_s[:, OFF[p] : OFF[p] + COLS[p]], preferred_element_type=F32)
            oo[p][i] = result.astype(BF).reshape(4, 4, 16, COLS[p])

    for i in STEPS:
        for p in range(3):
            arrived(rr[p].at[i], d_rs.at[p * 4 + i])
        expert_rows(i)
        come(0, i, 0)
        for b in (2, 1, 3, 0):
            k = i * 4 + b
            come(1, 1, k)
            come(2, 1, k)
            for k in ORDER[b * 4 : b * 4 + 4]:
                come(0, i, k)
    for k in (*ORDER, 0):
        for p in (1, 2):
            come(p, 0, k)

    x_in = {}

    def combine(p, d):
        sums = jnp.dot(
            com_s[p, d], rt[p][d].reshape(256, COLS[p]), preferred_element_type=F32
        ).reshape(2, 64, COLS[p])
        pf[p][d] = jnp.where(c == 0, sums[0], sums[1])
        px[p][d] = jnp.where(c == 0, sums[1], sums[0]).astype(BF)
        i = p * 4 + d
        x_in[p, d] = send(px[p].at[d], xr[p].at[d], x_ss.at[p], x_rs.at[i], dev(at, other))

    def give(p, d):
        x_in[p, d].wait_recv()
        total = pf[p][d] + xr[p][d].astype(F32)
        if d == 0:
            pf[p][d] = total
            return
        ps[p][d] = total.astype(BF)
        send(ps[p].at[d], pr[p].at[d], p_ss.at[p], p_rs.at[p], dev(along(p, d), c))

    for i in STEPS[:3]:
        arrived(rt0.at[i], e_rs.at[group(0, i)])
        combine(0, i)
    for d in STEPS[:3]:
        give(0, d)
    for p in (1, 2):
        arrived(rt[p].at[1:4], e_rs.at[group(p, 1)])
    for d in (2, 1, 3):
        for p in (1, 2):
            combine(p, d)
    for d in (2, 1, 3):
        for p in (1, 2):
            give(p, d)
    for p in range(3):
        arrived(rt[p].at[0], e_rs.at[group(p, 0)])
        combine(p, 0)
        drains.append((xr[p], x_ss.at[p]))
        drains.append((pr[p].at[1:4], p_ss.at[p]))
    for p in range(3):
        give(p, 0)
        arrived(pr[p].at[1:4], p_rs.at[p])
    for p in range(3):
        columns = slice(OFF[p], OFF[p] + COLS[p])
        total = pj_s[:, columns] + pf[p][0]
        for d in range(1, 4):
            total = total + pr[p][d].astype(F32)
        out_ref[:, columns] = total
    for ref, sem in drains:
        arrived(ref, sem)


def layer(queries, key_rows, values, out_weight, expert_ids, gate_ints, w_gate, w_up, w_down):
    count = queries.shape[0] // CHUNK
    blocks = [a.reshape(count, CHUNK, 128) for a in (queries, key_rows, values)]
    vm = pltpu.VMEM
    sem = lambda n: pltpu.SemaphoreType.DMA((n,))
    by = lambda *lead: [vm((*lead, n), BF) for n in COLS]
    scratch = [
        vm((count, CHUNK, 128), F32), vm((count, CHUNK, 128), F32), vm((count, CHUNK, 128), F32),
        vm((count, CHUNK, 128), F32), vm((128, 128), BF), vm((4, 128, 128), BF),
        vm((4, 2, 4, 64, 128), BF), vm((4, 2, 4, 64, 128), BF), vm((4, 2, 4, 64, 128), BF),
        vm((4, 2, 128, HALF), BF), vm((4, 2, 128, HALF), BF),
        vm((CB, 4, 64, CBW), BF), vm((CB, 4, 64, CBW), BF), vm((CB, 4, 64, CBW), F32), vm((64, 2048), F32),
        vm((16, 128), BF), vm((4, 2, 16, 128), BF), vm((4, 2, 16, 128), BF), vm((4, 2, 16, 128), BF),
        vm((3, 4, 256, 128), BF), vm((3, 4, 128, 256), BF),
        *by(4, 2, 64), *by(4, 16, 16), *by(4, 4, 4, 16), *by(4, 4, 4, 16), *by(4, 16, 16),
        *[vm((4, 64, n), F32) for n in COLS], *by(4, 64), *by(4, 64), *by(4, 64), *by(4, 64),
        vm((2048, 768), BF), vm((2048, 768), BF), vm((768, 2048), BF),
        sem(8), sem(1), sem(1), sem(3), sem(2), sem(2), sem(8), sem(4), sem(4), sem(1), sem(4),
        sem(6), sem(3), sem(6), sem(24), sem(8), sem(12), sem(8), sem(8),
        sem(3), sem(12), sem(3), sem(3), sem(2), sem(8), sem(2), sem(8),
    ]
    hbm = pl.BlockSpec(memory_space=pl.ANY)
    vmem = pl.BlockSpec(memory_space=pltpu.VMEM)
    return pl.pallas_call(
        body,
        out_shape=jax.ShapeDtypeStruct((64, 2048), F32),
        in_specs=[hbm, hbm, hbm, hbm, vmem, vmem, hbm, hbm, hbm],
        out_specs=vmem,
        scratch_shapes=scratch,
        compiler_params=pltpu.CompilerParams(
            collective_id=0, has_side_effects=True, vmem_limit_bytes=62 << 20
        ),
        cost_estimate=pl.CostEstimate(flops=13 * 10**9, bytes_accessed=14 * 10**6, transcendentals=10**6),
    )(*blocks, out_weight, expert_ids.T, gate_ints.T, w_gate[0], w_up[0], w_down[0])


def solution(mesh):
    placed = (
        P("seq", "head"),
        P("seq", "head"),
        P("seq", "head"),
        P("head", None),
        P(("seq", "head"), None),
        P(("seq", "head"), None),
        P(("seq", "head"), None, None),
        P(("seq", "head"), None, None),
        P(("seq", "head"), None, None),
    )
    return jax.shard_map(
        layer, mesh=mesh, in_specs=placed, out_specs=P(("seq", "head"), None), check_vma=False
    )
```
